32 devices in a mesh: tm: 16 (over z, x, core), space: 2 (over y).
Axes of the slice: x: 2, y: 2, z: 4, core: 2. Of those that a mesh axis runs over, the one named last changes fastest.
Arguments:
- adjoint: float32 [16, 5, 4, 4, 4, 256], P('tm', None, None, None, None, 'space'), may hold values from -6 to 6
- gradient: float32 [16, 5, 4, 4, 4, 256], P('tm', None, None, None, None, 'space'), may hold values from -6 to 6
- jacobian: float32 [16, 3, 5, 5, 4, 4, 4, 256], P('tm', None, None, None, None, None, None, 'space'), may hold values from -0.3 to 0.3
- pseudo_step: float32 [16, 256], P('tm', 'space'), may hold values from 0.05 to 0.2
- send_list: int32 [512], P('space'), may hold values from 0 to 767, as said below
- face_source: int32 [6, 256], P(None, 'space'), may hold values from 0 to 1024, as said below
- coarse_owner: int32 [256, 1], P('space'), may hold values from 0 to 1; in each aligned block of 128 rows (0 to 127, 128 to 255, ...) at most 96 rows name the same one
- coarse_inv: float32 [16, 40, 40, 384], P('tm', None, None, 'space')
Outputs:
- adjoint_next: float32 [16, 5, 4, 4, 4, 256], P('tm', None, None, None, None, 'space')
The draws below stay inside these ranges and needn't reach their ends.
Inputs may be any that keep to these rules, and one draw needn't show every extreme that they name: Each partition's face_source names slots of the previous and of the next partition's packed blocks for some of its faces; the rest of its faces take own columns or the zero column. `send_list`: entries are columns of the partition's own trace table. `coarse_owner`: at most 96 elements of one partition have the same owner; some owner receives exactly 96 from some partition.
All inputs are finite; a program needn't handle non-finite values.
Results may differ from the reference program's by a relative error of at most 0.0001.
Values sent between devices are 32-bit elements; how exact they have to be, the bound alone decides.
A program may use at most 64 MiB of HBM per device.

```python
import math
import jax
import jax.numpy as jnp
import numpy as np
from jax import lax

E_DEV = 128
NT = 16
NE = 256
SLOTS = 128
CAP = 96
N_SPACE = 2


def mesh_lists(key):
    faces_dev = 6 * E_DEV
    keys = jax.random.split(jax.random.fold_in(key, 4242), 6)
    lanes = jnp.arange(N_SPACE)
    from_prev = jax.random.randint(keys[0], (N_SPACE,), SLOTS // 3, SLOTS + 1)
    from_next = jax.random.randint(keys[1], (N_SPACE,), SLOTS // 3, SLOTS + 1)
    from_prev = jnp.where(lanes == jax.random.randint(keys[2], (), 0, N_SPACE), SLOTS, from_prev)
    from_next = jnp.where(lanes == jax.random.randint(keys[3], (), 0, N_SPACE), SLOTS, from_next)
    orders = jax.vmap(lambda sub_key: jax.random.permutation(sub_key, faces_dev))(jax.random.split(keys[4], N_SPACE))
    face_ids = orders // E_DEV
    source = (face_ids + 1 - 2 * (face_ids % 2)) * E_DEV + jax.random.randint(keys[5], (N_SPACE, faces_dev), 0, E_DEV)
    slot_ids = jnp.arange(SLOTS)[None, :]
    prev_src = jnp.where(slot_ids < from_prev[:, None], source[:, :SLOTS], 0)
    next_src = jnp.where(slot_ids < from_next[:, None], jnp.take_along_axis(source, from_prev[:, None] + slot_ids, axis=1), 0)
    send_list = jnp.concatenate([jnp.roll(next_src, 1, axis=0), jnp.roll(prev_src, -1, axis=0)], axis=1)
    ranks = jnp.argsort(orders, axis=1)
    local_src = jnp.take_along_axis(source, ranks, axis=1)
    base_col = 6 * E_DEV
    both = (from_prev + from_next)[:, None]
    lookup = jnp.where(ranks < from_prev[:, None], base_col + ranks, jnp.where(ranks < both, base_col + SLOTS + ranks - from_prev[:, None], jnp.where(ranks < both + E_DEV // 2, base_col + 2 * SLOTS, local_src)))
    face_source = lookup.reshape(N_SPACE, 6, E_DEV).transpose(1, 0, 2).reshape(6, N_SPACE * E_DEV)
    return (send_list.reshape(N_SPACE * 2 * SLOTS).astype(jnp.int32), face_source.astype(jnp.int32))


def draw_send_list(key, part):
    return mesh_lists(key)[0]


def draw_face_source(key, part):
    return mesh_lists(key)[1]


def draw_coarse_inv(key, part):
    layout = (NT, 40, 40, N_SPACE * N_SPACE * CAP)
    first_key, second_key = jax.random.split(jax.random.fold_in(key, 77))
    same = (jnp.arange(40)[:, None] == jnp.arange(40)[None, :]).astype(jnp.float32)[None, :, :, None]
    spread = 0.03 * jax.random.normal(first_key, layout, jnp.float32)
    diagonal = jax.random.uniform(second_key, layout, jnp.float32, 1.0, 1.5)
    spread = jnp.clip(spread, -0.09, 0.09)
    return (spread * (1.0 - same) + diagonal * same).astype(jnp.float32)


def block_levels(rng, dims, cuts, low, top_value):
    loudness = 1.0
    for dim, parts in cuts:
        heights = jax.random.uniform(jax.random.fold_in(jax.random.fold_in(rng, 6), dim), (parts,), jnp.float32, low / len(cuts), top_value / len(cuts))
        loudness = loudness * jnp.repeat(jnp.exp(heights), dims[dim] // parts).reshape((-1,) + (1,) * (len(dims) - 1 - dim))
    return loudness


def assign_block(own_key, own, number, rows, number_of, top, most, lean):
    ranking = jax.random.permutation(own_key, number_of)
    heavy_load, ordinary = shares(number_of, rows * top, most, lean, True), shares(number_of, rows * top, most, lean, False)
    places = jnp.arange(number_of)

    def named(lengths, turn):
        used = int((lengths > 0).sum())
        fixed = max(1, used // 4)
        passed = fixed + (places - fixed + turn * (used - fixed)) % max(1, number_of - fixed)
        return jnp.zeros((number_of,), jnp.int32).at[ranking[jnp.where(places < fixed, places, passed)]].set(jnp.asarray(lengths, jnp.int32))

    lengths = jnp.where(number % 4 == 0, named(heavy_load, number // 4), named(ordinary, number - number // 4 - 1))
    mixed = jax.random.permutation(jax.random.fold_in(own, 3), number_of)
    giver, taker = mixed[0:number_of // 2 * 2:2], mixed[1:number_of // 2 * 2:2]
    room = jnp.minimum(lengths[giver] - 1, most - lengths[taker]) // 2
    room = jnp.where((giver == ranking[0]) | (taker == ranking[0]) | (lengths[taker] == 0), 0, jnp.maximum(room, 0))
    passed = jax.random.randint(jax.random.fold_in(own, 4), (number_of // 2,), 0, 1 << 20) % (room + 1)
    lengths = lengths.at[giver].add(-passed).at[taker].add(passed)
    labels = jnp.searchsorted(jnp.cumsum(lengths), jnp.arange(rows * top), side="right").astype(jnp.int32)
    grid = labels.reshape(top, rows).T
    grid = grid[jax.random.permutation(jax.random.fold_in(own, 1), rows)]
    turn = jax.random.randint(jax.random.fold_in(own, 2), (rows, 1), 0, top)
    return jnp.take_along_axis(grid, (jnp.arange(top)[None, :] + turn) % top, axis=1)


def shares(count, total, limit, lean, full):
    loads = [(1 << 20) // math.isqrt(grade ** lean) + 1 for grade in range(1, count + 1)]
    largest = limit if full else min(limit, max(-(-total // count), total * loads[0] // sum(loads)))
    least = 1 if total - largest >= count - 1 else 0
    holding, rest = [largest] + [least] * (count - 1), total - largest - least * (count - 1)
    while rest > 0:
        free = [i for i in range(1, count) if holding[i] < largest] or [i for i in range(1, count) if holding[i] < limit]
        whole, remaining = sum([loads[i] for i in free]), rest
        for i in free:
            extra = min(limit - holding[i], max(1, remaining * loads[i] // whole), rest)
            holding[i] = holding[i] + extra
            rest = rest - extra
    return np.array(holding)


def bell_draw(stream_key, extent, deviation, reach, cuts=(), kind=jnp.bfloat16):
    values = deviation * jax.random.normal(stream_key, extent, jnp.float32)
    if cuts:
        values = values * block_levels(stream_key, extent, cuts, -0.22, 0.18)
    return jnp.clip(values, -reach, reach).astype(kind)


def setup_inputs(seed: int = 0) -> dict:
    arg_keys = jax.random.split(jax.random.key(seed), 9)
    adjoint = bell_draw(arg_keys[0], (NT, 5, 4, 4, 4, NE), 1.0, 6.0, ((0, 16), (5, 2)), jnp.float32)
    gradient = bell_draw(arg_keys[1], (NT, 5, 4, 4, 4, NE), 1.0, 6.0, ((0, 16), (5, 2)), jnp.float32)
    jacobian = bell_draw(arg_keys[2], (NT, 3, 5, 5, 4, 4, 4, NE), 0.05, 0.3, ((0, 16), (7, 2)), jnp.float32)
    pseudo_step = jnp.clip(jnp.exp(math.log(0.2) - 1.3862944 * jax.random.uniform(arg_keys[3], (NT, NE), jnp.float32) ** block_levels(arg_keys[3], (NT, NE), ((0, 16), (1, 2)), -0.2, 0.2)), 0.05, 0.2)
    send_list = draw_send_list(jax.random.fold_in(arg_keys[8], 71), 0)
    face_source = draw_face_source(jax.random.fold_in(arg_keys[8], 71), 0)
    coarse_owner_keys = jax.random.split(jax.random.fold_in(arg_keys[6], 1), NE // E_DEV)
    coarse_owner_turns = jax.random.permutation(jax.random.fold_in(arg_keys[6], 3), NE // E_DEV)
    coarse_owner = jax.vmap(lambda own, number: assign_block(jax.random.fold_in(arg_keys[6], 2), own, number, E_DEV, N_SPACE, 1, CAP, 2))(coarse_owner_keys, coarse_owner_turns).reshape((NE, 1))
    coarse_inv = draw_coarse_inv(jax.random.fold_in(arg_keys[8], 71), 0)
    return {"adjoint": adjoint, "gradient": gradient, "jacobian": jacobian, "pseudo_step": pseudo_step, "send_list": send_list, "face_source": face_source, "coarse_owner": coarse_owner, "coarse_inv": coarse_inv}


freq_scale = 0.25
relax_rate = 2.0
penalty = 1.0
highest = lax.Precision.HIGHEST
einsum_forms = ("km,...kbce->...mbce", "km,...akce->...amce", "km,...abke->...abme")


def node_points(n):
    return np.linspace(-1.0, 1.0, n)


def lagrange(anchor, target):
    matrix = np.ones((len(target), len(anchor)))
    for c in range(len(anchor)):
        for k in range(len(anchor)):
            if k != c:
                matrix[:, c] = matrix[:, c] * (target - anchor[k]) / (anchor[c] - anchor[k])
    return matrix


def derivative(n):
    points = node_points(n)
    weights = np.ones(n)
    for j in range(n):
        for k in range(n):
            if k != j:
                weights[j] = weights[j] / (points[j] - points[k])
    matrix = np.zeros((n, n))
    for i in range(n):
        for j in range(n):
            if i != j:
                matrix[i, j] = weights[j] / weights[i] / (points[i] - points[j])
        matrix[i, i] = -np.sum(matrix[i])
    return jnp.asarray(matrix, jnp.float32)


def along_axis(matrix, values, axis_id):
    return jnp.einsum(einsum_forms[axis_id], matrix, values, precision=highest)


def restrict(values, matrix):
    for axis_id in range(3):
        values = along_axis(matrix, values, axis_id)
    return values


def prolong(values, matrix):
    for axis_id in range(3):
        values = along_axis(matrix.T, values, axis_id)
    return values


def coupling(count):
    offsets = (jnp.arange(count)[:, None] - jnp.arange(count)[None, :]) % count
    angles = jnp.pi * offsets.astype(jnp.float32) / count
    parity = (1 - 2 * (offsets % 2)).astype(jnp.float32)
    safe_sin = jnp.where(offsets == 0, 1.0, jnp.sin(angles))
    spectral = jnp.where(offsets == 0, 0.0, 0.5 * parity * jnp.cos(angles) / safe_sin)
    same = (offsets == 0).astype(jnp.float32)
    return freq_scale * spectral + relax_rate * (same - 1.0 / count)


def face_take(values, face_id, n):
    return jnp.take(values, (face_id % 2) * (n - 1), axis=values.ndim - 4 + face_id // 2)


def face_put(values, face_id, n, addend):
    lookup = [slice(None)] * values.ndim
    lookup[values.ndim - 4 + face_id // 2] = (face_id % 2) * (n - 1)
    return values.at[tuple(lookup)].add(addend)


def per_part(matrix, lookup):
    return jax.vmap(lambda part_tab, part_idx: jnp.take(part_tab, part_idx, axis=2), in_axes=(2, 0), out_axes=2)(matrix, lookup)


def trace_table(values, n):
    pieces = [face_take(values, face_id, n).reshape(NT, 5 * n * n, N_SPACE, 1, E_DEV) for face_id in range(6)]
    return jnp.concatenate(pieces, axis=3).reshape(NT, 5 * n * n, N_SPACE, 6 * E_DEV)


def neighbour_traces(own_traces, send_list, face_source):
    blocks = per_part(own_traces, send_list.reshape(N_SPACE, 2 * SLOTS))
    from_prev = jnp.roll(blocks, 1, axis=2)[:, :, :, SLOTS:]
    from_next = jnp.roll(blocks, -1, axis=2)[:, :, :, :SLOTS]
    zero_col = jnp.zeros(blocks.shape[:3] + (1,), blocks.dtype)
    combined = jnp.concatenate([own_traces, from_prev, from_next, zero_col], axis=3)
    lookup = face_source.reshape(6, N_SPACE, E_DEV).transpose(1, 0, 2).reshape(N_SPACE, 6 * E_DEV)
    return per_part(combined, lookup)


def operator(values, jacobian, n, send_list, face_source, mixing):
    matrix = derivative(n)
    summed = jnp.zeros_like(values)
    for axis_id in range(3):
        flux_terms = jnp.einsum("...ijabce,...iabce->...jabce", jacobian[:, axis_id], values, precision=highest)
        summed = summed + along_axis(matrix, flux_terms, axis_id)
    trace_width = 5 * n * n
    own_traces = trace_table(values, n)
    far_traces = neighbour_traces(own_traces, send_list, face_source)
    jump_terms = (own_traces - far_traces).reshape(NT, trace_width, N_SPACE, 6, E_DEV)
    for face_id in range(6):
        summed = face_put(summed, face_id, n, penalty * jump_terms[:, :, :, face_id, :].reshape(NT, 5, n, n, NE))
    return summed + jnp.einsum("st,s...->t...", mixing, values, precision=highest)


def coarse_solve(low_rhs, coarse_owner, coarse_inv):
    flattened = low_rhs.reshape(NT, 40, NE)
    owners = coarse_owner.reshape(N_SPACE, E_DEV)
    one_hot = (owners[:, :, None] == jnp.arange(N_SPACE)[None, None, :]).astype(jnp.int32)
    before = jnp.cumsum(one_hot, axis=1) - one_hot
    rank_pos = jnp.sum(before * one_hot, axis=2)
    column = owners * (N_SPACE * CAP) + jnp.arange(N_SPACE)[:, None] * CAP + rank_pos
    blocks = jnp.take(coarse_inv, column.reshape(NE).astype(jnp.int32), axis=3)
    solved = jnp.einsum("tije,tje->tie", blocks, flattened, precision=highest)
    return solved.reshape(NT, 5, 2, 2, 2, NE)


def scaled(step_size, values):
    return step_size[:, None, None, None, None, :] * values


def reference(adjoint, gradient, jacobian, pseudo_step, send_list, face_source, coarse_owner, coarse_inv):
    mixing = coupling(NT)
    fine_to_mid = jnp.asarray(lagrange(node_points(3), node_points(4)), jnp.float32)
    mid_to_low = jnp.asarray(lagrange(node_points(2), node_points(3)), jnp.float32)
    sample = jnp.asarray(lagrange(node_points(4), node_points(3)).T, jnp.float32)
    jac_mid = restrict(jacobian, sample)

    def apply_fine(values):
        return operator(values, jacobian, 4, send_list, face_source, mixing)

    def apply_mid(values):
        return operator(values, jac_mid, 3, send_list, face_source, mixing)

    residual = gradient - apply_fine(adjoint)
    smoothed = adjoint + scaled(pseudo_step, residual)
    residual = gradient - apply_fine(smoothed)
    coarse_rhs = restrict(residual, fine_to_mid)
    correction = scaled(pseudo_step, coarse_rhs)
    correction = correction + scaled(pseudo_step, coarse_rhs - apply_mid(correction))
    mid_residual = coarse_rhs - apply_mid(correction)
    low_rhs = restrict(mid_residual, mid_to_low)
    low_fix = coarse_solve(low_rhs, coarse_owner, coarse_inv)
    correction = correction + prolong(low_fix, mid_to_low)
    correction = correction + scaled(pseudo_step, coarse_rhs - apply_mid(correction))
    corrected = smoothed + prolong(correction, fine_to_mid)
    return corrected + scaled(pseudo_step, gradient - apply_fine(corrected))
```

```python
import functools

import jax
import jax.numpy as jnp
import ml_dtypes
import numpy as np
from jax import lax
from jax.experimental import pallas as pl
from jax.experimental.pallas import tpu as pltpu
from jax.sharding import PartitionSpec as P

MESH = pl.DeviceIdType.MESH
f32, bf16 = jnp.float32, jnp.bfloat16
LANES = 128


def node_points(n):
    return np.linspace(-1.0, 1.0, n)


def lagrange(anchor, target):
    matrix = np.ones((len(target), len(anchor)))
    for c in range(len(anchor)):
        for k in range(len(anchor)):
            if k != c:
                matrix[:, c] = matrix[:, c] * (target - anchor[k]) / (anchor[c] - anchor[k])
    return matrix


def derivative(n):
    points = node_points(n)
    weights = np.ones(n)
    for j in range(n):
        for k in range(n):
            if k != j:
                weights[j] = weights[j] / (points[j] - points[k])
    matrix = np.zeros((n, n))
    for i in range(n):
        for j in range(n):
            if i != j:
                matrix[i, j] = weights[j] / weights[i] / (points[i] - points[j])
        matrix[i, i] = -np.sum(matrix[i])
    return matrix


def coupling_row(count):
    row = []
    for k in range(count):
        d = 0.0 if k == 0 else 0.5 * (-1) ** k * np.cos(np.pi * k / count) / np.sin(np.pi * k / count)
        row.append(float(0.25 * d + 2.0 * ((k == 0) - 1.0 / count)))
    return row


def kron3(a, b, c):
    return np.kron(np.kron(a, b), c)


def pad_to(matrix, rows, cols):
    out = np.zeros((rows, cols))
    out[: matrix.shape[0], : matrix.shape[1]] = matrix
    return out


def split_cat(matrix):
    hi = matrix.astype(np.float32).astype(ml_dtypes.bfloat16)
    lo = (matrix.astype(np.float32) - hi.astype(np.float32)).astype(ml_dtypes.bfloat16)
    return np.concatenate([hi, lo, hi], axis=1)


def face_select(n, rows):
    select = np.zeros((96, rows))
    for f in range(6):
        axis, end = f // 2, (f % 2) * (n - 1)
        count = 0
        for r in range(n):
            for s in range(n):
                index = [r, s]
                index.insert(axis, end)
                select[16 * f + count, (index[0] * n + index[1]) * n + index[2]] = 1.0
                count += 1
    return select


def deriv_cat(n, rows):
    dt, one = derivative(n).T, np.eye(n)
    return np.concatenate(
        [pad_to(m, rows, rows) for m in (kron3(dt, one, one), kron3(one, dt, one), kron3(one, one, dt))],
        axis=1,
    )


@functools.cache
def constants():
    p43 = lagrange(node_points(3), node_points(4))
    p32 = lagrange(node_points(2), node_points(3))
    q34 = lagrange(node_points(4), node_points(3))
    p43k, p32k, q34k = kron3(p43, p43, p43), kron3(p32, p32, p32), kron3(q34, q34, q34)
    e4, e3 = face_select(4, 64), face_select(3, 32)
    tables = {
        "e4": e4,
        "e3": e3,
        "d4": split_cat(deriv_cat(4, 64)),
        "d3": split_cat(deriv_cat(3, 32)),
        "et4": np.concatenate([e4.T, e4.T], axis=1),
        "et3": np.concatenate([e3.T, e3.T], axis=1),
        "r43": split_cat(pad_to(p43k.T, 32, 64)),
        "p43": split_cat(pad_to(p43k, 64, 32)),
        "r32": split_cat(pad_to(p32k.T, 16, 32)),
        "p32": split_cat(pad_to(p32k, 32, 8)),
        "q34": split_cat(pad_to(q34k, 32, 64)),
    }
    where, pieces, at = {}, [], 0
    for name, table in tables.items():
        where[name] = (at, table.shape[0], table.shape[1])
        pieces.append(pad_to(table.astype(np.float64), table.shape[0], 640))
        at += table.shape[0]
    return where, np.concatenate(pieces, axis=0).astype(ml_dtypes.bfloat16)


def dot(a, b):
    return jnp.dot(a, b, preferred_element_type=f32)


def split(x):
    hi = x.astype(bf16)
    return hi, (x - hi.astype(f32)).astype(bf16)


def split_rows(x):
    hi, lo = split(x)
    return jnp.concatenate([hi, hi, lo], axis=0)


def lane_cat(parts):
    return jnp.concatenate(parts, axis=1)


def kernel(nt, parts, cap, where, row, *refs):
    (adj, grad, jac, tau_ref, send_ref, face_ref, owner_ref, inv, const, out,
     jm, pick, jump_w, far_w, pack_w, rows_f, rows_m, sol, *rest) = refs
    fine_t = [rest[4 * i:4 * i + 4] for i in range(2)]
    mid_t = [rest[8 + 4 * i:12 + 4 * i] for i in range(5)]
    trace_out, trace_in, low_out, low_in, low_back = rest[28:33]
    t_send, t_recv, b_send, b_recv, h_send, h_recv, c_send, c_recv, g_send, g_recv = rest[33:]
    me_t, me_s = lax.axis_index("tm"), lax.axis_index("space")
    columns = LANES
    width = 5 * columns
    slots = send_ref.shape[1] // 2
    faces = 6 * columns
    cols = inv.shape[2]

    def mat(name):
        at, height, wide = where[name]
        return const[at:at + height, 0:wide]

    barrier = pltpu.get_barrier_semaphore()
    for k in range(1, nt):
        pl.semaphore_signal(barrier, inc=1, device_id={"tm": lax.rem(me_t + k, nt)}, device_id_type=MESH)
    for k in range(1, parts):
        pl.semaphore_signal(barrier, inc=1, device_id={"space": lax.rem(me_s + k, parts)}, device_id_type=MESH)
    pl.semaphore_wait(barrier, nt - 1 + parts - 1)

    def t_start(number, bufs, v):
        stage, landed, mixed, back = bufs
        piece = stage.shape[1]
        for k in range(nt):
            stage[k] = v[piece * k:piece * (k + 1), :]
        for k in range(1, nt):
            to = lax.rem(me_t + k, nt)
            pltpu.make_async_remote_copy(
                src_ref=stage.at[to], dst_ref=landed.at[nt - k], send_sem=t_send.at[number],
                recv_sem=t_recv.at[number], device_id={"tm": to}, device_id_type=MESH).start()
        landed[0] = stage[me_t]

    def all_of(buf, sem):
        view = buf.at[pl.ds(1, nt - 1)]
        pltpu.make_async_copy(view, view, sem).wait()

    def t_mix(number, bufs):
        stage, landed, mixed, back = bufs
        all_of(landed, t_recv.at[number])

        def block(b, carry):
            lanes = pl.ds(pl.multiple_of(b * LANES, LANES), LANES)
            y = landed[:, :, lanes]
            total = row[0] * y
            for m in range(1, nt):
                total = total + row[m] * jnp.concatenate([y[m:], y[:m]], axis=0)
            mixed[:, :, lanes] = total
            return carry

        lax.fori_loop(0, width // LANES, block, 0)
        for k in range(1, nt):
            to = lax.rem(me_t + k, nt)
            pltpu.make_async_remote_copy(
                src_ref=mixed.at[k], dst_ref=back.at[me_t], send_sem=b_send.at[number],
                recv_sem=b_recv.at[number], device_id={"tm": to}, device_id_type=MESH).start()
        back[me_t] = mixed[0]

    def t_finish(number, bufs, rows_ref):
        stage, landed, mixed, back = bufs
        all_of(back, b_recv.at[number])
        piece = stage.shape[1]
        for k in range(nt):
            rows_ref[piece * k:piece * (k + 1), :] = back[k]
        return rows_ref[...]

    def trace_copy(number, side):
        to = lax.rem(me_s + (parts - 1 if side == 0 else 1), parts)
        return pltpu.make_async_remote_copy(
            src_ref=trace_out.at[number, side], dst_ref=trace_in.at[number, 1 - side],
            send_sem=h_send.at[number, side], recv_sem=h_recv.at[number, 1 - side],
            device_id={"space": to}, device_id_type=MESH)

    def s_start(number, v, e_name):
        hi, lo = split(v)
        chosen = mat(e_name)
        t_hi, t_lo = dot(chosen, hi).astype(bf16), dot(chosen, lo).astype(bf16)
        table = jnp.concatenate(
            [lane_cat([t[16 * f:16 * f + 16, columns * i:columns * (i + 1)] for f in range(6)])
             for t in (t_hi, t_lo) for i in range(5)], axis=0)
        packed = dot(table, pick[...])
        packed = packed[:80] + packed[80:]
        for side in range(2):
            trace_out[number, side] = packed[:, slots * side:slots * (side + 1)]
            trace_copy(number, side).start()
        return table

    def flux(v, jac_at, d_name):
        w = []
        for a in range(3):
            total = jac_at[5 * a] * v[:, 0:columns][None]
            for i in range(1, 5):
                total = total + jac_at[5 * a + i] * v[:, columns * i:columns * (i + 1)][None]
            w.append(lane_cat([total[j] for j in range(5)]))
        return dot(mat(d_name), split_rows(jnp.concatenate(w, axis=0)))

    def s_local(table):
        jump = dot(table, jump_w[...])
        return jump[:80] + jump[80:]

    def s_finish(number, jump, et_name):
        for side in range(2):
            trace_copy(number, side).wait_recv()
        hi, lo = split(lane_cat([trace_in[number, 0], trace_in[number, 1]]))
        far = dot(jnp.concatenate([hi, lo], axis=0), far_w[...])
        jump = jump + far[:80] + far[80:]
        put = jnp.concatenate(
            [lane_cat([jump[16 * i:16 * i + 16, columns * f:columns * (f + 1)] for i in range(5)])
             for f in range(6)], axis=0)
        hi, lo = split(put)
        return dot(mat(et_name), jnp.concatenate([hi, lo], axis=0))

    v = lane_cat([adj[i] for i in range(5)])
    t_start(0, fine_t[0], v)
    rows768 = lax.broadcasted_iota(jnp.int32, (faces, 2 * slots), 0)
    pick[...] = jnp.where(rows768 == send_ref[...], 1.0, 0.0).astype(bf16)
    table = s_start(0, v, "e4")
    row_id = lax.broadcasted_iota(jnp.int32, (faces, columns), 0)
    lane_id = lax.broadcasted_iota(jnp.int32, (faces, columns), 1)
    far_id = lax.broadcasted_iota(jnp.int32, (2 * slots, columns), 0) + faces
    for f in range(6):
        source = face_ref[f:f + 1, :]
        own = jnp.where(row_id == lane_id + f * columns, 1.0, 0.0)
        jump_w[:, columns * f:columns * (f + 1)] = (own - jnp.where(row_id == source, 1.0, 0.0)).astype(bf16)
        far_w[:, columns * f:columns * (f + 1)] = jnp.where(far_id == source, -1.0, 0.0).astype(bf16)
    tau = lane_cat([tau_ref[...]] * 5)
    g = lane_cat([grad[i] for i in range(5)])
    part = flux(v, jac, "d4")
    jump = s_local(table)
    t_mix(0, fine_t[0])
    part = g - part - s_finish(0, jump, "et4")

    def to_mid(c, carry):
        picked = lane_cat([jac[c, j] for j in range(5)])
        small = dot(mat("q34"), split_rows(picked))
        for j in range(5):
            jm[c, j] = small[:, columns * j:columns * (j + 1)]
        return carry

    lax.fori_loop(0, 15, to_mid, 0)
    owners = owner_ref[...]
    lane_c = lax.broadcasted_iota(jnp.int32, (columns, LANES), 1)
    sub_c = lax.broadcasted_iota(jnp.int32, (columns, LANES), 0)
    named = jnp.where(owners == lane_c, 1.0, 0.0)
    before = dot(jnp.where(sub_c > lane_c, 1.0, 0.0).astype(bf16), named.astype(bf16))
    rank = jnp.sum(before * named, axis=1, keepdims=True)
    wide = pack_w.shape[2]
    lane_w = lax.broadcasted_iota(jnp.int32, (columns, wide), 1).astype(f32)
    slot = rank + (me_s * cap).astype(f32)
    for q in range(parts):
        pack_w[q] = jnp.where(jnp.logical_and(lane_w == slot, owners == q), 1.0, 0.0).astype(bf16)

    smoothed = v + tau * (part - t_finish(0, fine_t[0], rows_f))

    t_start(1, mid_t[0], dot(mat("r43"), split_rows(smoothed)))
    table = s_start(1, smoothed, "e4")
    t_start(2, fine_t[1], smoothed)
    part = flux(smoothed, jac, "d4")
    jump = s_local(table)
    t_mix(1, mid_t[0])
    part = g - part - s_finish(1, jump, "et4")
    rhs = dot(mat("r43"), split_rows(part)) - t_finish(1, mid_t[0], rows_m)

    def mid_residual(number, t_number, bufs, c, background=None):
        t_start(t_number, bufs, c)
        made = s_start(number, c, "e3")
        inner = flux(c, jm, "d3")
        step_jump = s_local(made)
        t_mix(t_number, bufs)
        if background is not None:
            background()
        inner = rhs - inner - s_finish(number, step_jump, "et3")
        return inner - t_finish(t_number, bufs, rows_m)

    c = tau * rhs
    c = c + tau * mid_residual(2, 3, mid_t[1], c, lambda: t_mix(2, fine_t[1]))
    left = mid_residual(3, 4, mid_t[2], c)

    low = dot(mat("r32"), split_rows(left))[:8]
    low = jnp.concatenate([low[:, columns * i:columns * (i + 1)] for i in range(5)], axis=0)
    hi, lo = split(low)
    stacked = jnp.concatenate([hi, lo], axis=0)

    def packed_for(q):
        both = dot(stacked, pack_w[q])
        return both[:40] + both[40:]

    def low_copy(k):
        return pltpu.make_async_remote_copy(
            src_ref=low_out.at[k], dst_ref=low_in.at[parts - k], send_sem=c_send.at[k],
            recv_sem=c_recv.at[parts - k], device_id={"space": lax.rem(me_s + k, parts)}, device_id_type=MESH)

    def back_copy(k):
        return pltpu.make_async_remote_copy(
            src_ref=sol, dst_ref=low_back.at[parts - k], send_sem=g_send.at[k],
            recv_sem=g_recv.at[parts - k], device_id={"space": lax.rem(me_s + k, parts)}, device_id_type=MESH)

    for k in range(1, parts):
        low_out[k] = packed_for(lax.rem(me_s + k, parts))
        low_copy(k).start()
    arrived = packed_for(me_s)
    for k in range(1, parts):
        low_copy(k).wait_recv()
    for k in range(1, parts):
        arrived = arrived + low_in[k]
    arrived = arrived[:, :cols]
    if wide > cols:
        sol[:, cols:] = jnp.zeros((40, wide - cols), f32)
    for i in range(40):
        sol[i:i + 1, :cols] = jnp.sum(inv[i] * arrived, axis=0, keepdims=True)
    for k in range(1, parts):
        back_copy(k).start()

    def unpacked(values, q):
        v_hi, v_lo = split(values)
        both = lax.dot_general(
            jnp.concatenate([v_hi, v_lo], axis=0), pack_w[q], (((1,), (1,)), ((), ())),
            preferred_element_type=f32)
        return both[:40] + both[40:]

    fix = unpacked(sol[...], me_s)
    for k in range(1, parts):
        back_copy(k).wait_recv()
    for k in range(1, parts):
        fix = fix + unpacked(low_back[k], lax.rem(me_s + k, parts))
    fix = lane_cat([fix[8 * i:8 * i + 8] for i in range(5)])
    hi = fix.astype(bf16).astype(f32)
    fix = jnp.concatenate([hi, hi, fix - hi], axis=0).astype(bf16)
    c = c + dot(mat("p32"), fix)

    c = c + tau * mid_residual(4, 5, mid_t[3], c)
    t_start(6, mid_t[4], c)
    corrected = smoothed + dot(mat("p43"), split_rows(c))
    table = s_start(5, corrected, "e4")
    part = flux(corrected, jac, "d4")
    jump = s_local(table)
    t_mix(6, mid_t[4])
    part = g - part - s_finish(5, jump, "et4")
    part = part - t_finish(2, fine_t[1], rows_f)
    coupled = dot(mat("p43"), split_rows(t_finish(6, mid_t[4], rows_m)))
    result = corrected + tau * (part - coupled)
    for i in range(5):
        out[i] = result[:, columns * i:columns * (i + 1)]

    order = [fine_t[0], mid_t[0], fine_t[1], mid_t[1], mid_t[2], mid_t[3], mid_t[4]]
    for number, bufs in enumerate(order):
        all_of(bufs[0], t_send.at[number])
        all_of(bufs[2], b_send.at[number])
    for number in range(6):
        for side in range(2):
            trace_copy(number, side).wait_send()
    for k in range(1, parts):
        low_copy(k).wait_send()
        back_copy(k).wait_send()


def on_device(nt, parts, where, table, row, adjoint, gradient, jacobian, pseudo_step, send_list,
              face_source, coarse_owner, coarse_inv):
    columns = adjoint.shape[-1]
    cols = coarse_inv.shape[-1]
    slots = send_list.shape[0] // 2
    wide = -(-cols // LANES) * LANES
    width = 5 * columns
    faces = 6 * columns
    vmem = pl.BlockSpec(memory_space=pltpu.VMEM)

    def time_buffers(rows):
        return [pltpu.VMEM((nt, rows // nt, width), f32) for _ in range(4)]

    scratch = [
        pltpu.VMEM((15, 5, 32, columns), f32),
        pltpu.VMEM((faces, 2 * slots), bf16),
        pltpu.VMEM((faces, faces), bf16),
        pltpu.VMEM((2 * slots, faces), bf16),
        pltpu.VMEM((parts, columns, wide), bf16),
        pltpu.VMEM((64, width), f32),
        pltpu.VMEM((32, width), f32),
        pltpu.VMEM((40, wide), f32),
    ]
    for rows in (64, 64, 32, 32, 32, 32, 32):
        scratch += time_buffers(rows)
    scratch += [
        pltpu.VMEM((6, 2, 80, slots), f32),
        pltpu.VMEM((6, 2, 80, slots), f32),
        pltpu.VMEM((parts, 40, wide), f32),
        pltpu.VMEM((parts, 40, wide), f32),
        pltpu.VMEM((parts, 40, wide), f32),
    ]
    dma = pltpu.SemaphoreType.DMA
    scratch += [dma((7,)) for _ in range(4)] + [dma((6, 2)) for _ in range(2)]
    scratch += [dma((parts,)) for _ in range(4)]
    result = pl.pallas_call(
        functools.partial(kernel, nt, parts, cols // parts, where, row),
        out_shape=jax.ShapeDtypeStruct((5, 64, columns), f32),
        in_specs=[vmem] * 9,
        out_specs=vmem,
        scratch_shapes=scratch,
        compiler_params=pltpu.CompilerParams(
            collective_id=0, has_side_effects=True, vmem_limit_bytes=50 * 1024 * 1024),
    )(
        adjoint.reshape(5, 64, columns),
        gradient.reshape(5, 64, columns),
        jacobian.reshape(15, 5, 64, columns),
        pseudo_step,
        send_list.reshape(1, 2 * slots),
        face_source,
        coarse_owner,
        coarse_inv.reshape(40, 40, cols),
        jnp.asarray(table),
    )
    return result.reshape(adjoint.shape)


def solution(mesh):
    nt, parts = mesh.shape["tm"], mesh.shape["space"]
    where, table = constants()
    placed = (
        P("tm", None, None, None, None, "space"),
        P("tm", None, None, None, None, "space"),
        P("tm", None, None, None, None, None, None, "space"),
        P("tm", "space"),
        P("space"),
        P(None, "space"),
        P("space", None),
        P("tm", None, None, "space"),
    )
    return jax.shard_map(
        functools.partial(on_device, nt, parts, where, table, coupling_row(nt)),
        mesh=mesh,
        in_specs=placed,
        out_specs=P("tm", None, None, None, None, "space"),
        check_vma=False,
    )
```

```python
import functools

import jax
import jax.numpy as jnp
import ml_dtypes
import numpy as np
from jax import lax
from jax.experimental import pallas as pl
from jax.experimental.pallas import tpu as pltpu
from jax.sharding import PartitionSpec as P

MESH = pl.DeviceIdType.MESH
f32, bf16 = jnp.float32, jnp.bfloat16
LANES = 128


def node_points(n):
    return np.linspace(-1.0, 1.0, n)


def lagrange(anchor, target):
    matrix = np.ones((len(target), len(anchor)))
    for c in range(len(anchor)):
        for k in range(len(anchor)):
            if k != c:
                matrix[:, c] = matrix[:, c] * (target - anchor[k]) / (anchor[c] - anchor[k])
    return matrix


def derivative(n):
    points = node_points(n)
    weights = np.ones(n)
    for j in range(n):
        for k in range(n):
            if k != j:
                weights[j] = weights[j] / (points[j] - points[k])
    matrix = np.zeros((n, n))
    for i in range(n):
        for j in range(n):
            if i != j:
                matrix[i, j] = weights[j] / weights[i] / (points[i] - points[j])
        matrix[i, i] = -np.sum(matrix[i])
    return matrix


def coupling_row(count):
    row = []
    for k in range(count):
        d = 0.0 if k == 0 else 0.5 * (-1) ** k * np.cos(np.pi * k / count) / np.sin(np.pi * k / count)
        row.append(float(0.25 * d + 2.0 * ((k == 0) - 1.0 / count)))
    return row


def kron3(a, b, c):
    return np.kron(np.kron(a, b), c)


def pad_to(matrix, rows, cols):
    out = np.zeros((rows, cols))
    out[: matrix.shape[0], : matrix.shape[1]] = matrix
    return out


def split_cat(matrix):
    hi = matrix.astype(np.float32).astype(ml_dtypes.bfloat16)
    lo = (matrix.astype(np.float32) - hi.astype(np.float32)).astype(ml_dtypes.bfloat16)
    return np.concatenate([hi, lo, hi], axis=1)


def face_select(n, rows):
    select = np.zeros((96, rows))
    for f in range(6):
        axis, end = f // 2, (f % 2) * (n - 1)
        count = 0
        for r in range(n):
            for s in range(n):
                index = [r, s]
                index.insert(axis, end)
                select[16 * f + count, (index[0] * n + index[1]) * n + index[2]] = 1.0
                count += 1
    return select


def deriv_cat(n, rows):
    dt, one = derivative(n).T, np.eye(n)
    return np.concatenate(
        [pad_to(m, rows, rows) for m in (kron3(dt, one, one), kron3(one, dt, one), kron3(one, one, dt))],
        axis=1,
    )


@functools.cache
def constants():
    p43 = lagrange(node_points(3), node_points(4))
    p32 = lagrange(node_points(2), node_points(3))
    q34 = lagrange(node_points(4), node_points(3))
    p43k, p32k, q34k = kron3(p43, p43, p43), kron3(p32, p32, p32), kron3(q34, q34, q34)
    e4, e3 = face_select(4, 64), face_select(3, 32)
    tables = {
        "e4": e4,
        "e3": e3,
        "d4": split_cat(deriv_cat(4, 64)),
        "d3": split_cat(deriv_cat(3, 32)),
        "et4": np.concatenate([e4.T, e4.T], axis=1),
        "et3": np.concatenate([e3.T, e3.T], axis=1),
        "r43": split_cat(pad_to(p43k.T, 32, 64)),
        "p43": split_cat(pad_to(p43k, 64, 32)),
        "r32": split_cat(pad_to(p32k.T, 16, 32)),
        "p32": split_cat(pad_to(p32k, 32, 8)),
        "q34": split_cat(pad_to(q34k, 32, 64)),
    }
    where, pieces, at = {}, [], 0
    for name, table in tables.items():
        where[name] = (at, table.shape[0], table.shape[1])
        pieces.append(pad_to(table.astype(np.float64), table.shape[0], 640))
        at += table.shape[0]
    return where, np.concatenate(pieces, axis=0).astype(ml_dtypes.bfloat16)


def dot(a, b):
    return jnp.dot(a, b, preferred_element_type=f32)


def split(x):
    hi = x.astype(bf16)
    return hi, (x - hi.astype(f32)).astype(bf16)


def split_rows(x):
    hi, lo = split(x)
    return jnp.concatenate([hi, hi, lo], axis=0)


def lane_cat(parts):
    return jnp.concatenate(parts, axis=1)


def kernel(nt, parts, cap, where, row, *refs):
    sources, out, held = refs[:9], refs[9], refs[10:19]
    adj, grad, jac, tau_ref, send_ref, face_ref, owner_ref, inv, const = held
    in_sem = refs[19]
    (jm, pick, jump_w, far_w, pack_w, rows_f, rows_m, rows_l, sol, *rest) = refs[20:]
    bufs_t = [rest[4 * i:4 * i + 4] for i in range(8)]
    trace_out, trace_in, low_out, low_in, low_back = rest[32:37]
    t_send, t_recv, b_send, b_recv, h_send, h_recv, c_send, c_recv, g_send, g_recv = rest[37:]
    me_t, me_s = lax.axis_index("tm"), lax.axis_index("space")
    columns = LANES
    width = 5 * columns
    slots = send_ref.shape[1] // 2
    faces = 6 * columns
    cols = inv.shape[2]

    far_first = sorted(range(1, nt), key=lambda k: (-min(k, nt - k), k))

    def mat(name):
        at, height, wide = where[name]
        return const[at:at + height, 0:wide]

    def fetch(i):
        return pltpu.make_async_copy(sources[i], held[i], in_sem.at[i])

    for i in (0, 4, 8, 5, 2, 1, 3, 6, 7):
        fetch(i).start()
    barrier = pltpu.get_barrier_semaphore()
    for k in range(1, nt):
        pl.semaphore_signal(barrier, inc=1, device_id={"tm": lax.rem(me_t + k, nt)}, device_id_type=MESH)
    for k in range(1, parts):
        pl.semaphore_signal(barrier, inc=1, device_id={"space": lax.rem(me_s + k, parts)}, device_id_type=MESH)
    fetch(0).wait()
    pl.semaphore_wait(barrier, nt - 1 + parts - 1)

    def t_start(number, v):
        stage, landed, mixed, back = bufs_t[number]
        piece = stage.shape[1]
        for k in range(nt):
            stage[k] = v[piece * k:piece * (k + 1), :]
        for k in far_first:
            to = lax.rem(me_t + k, nt)
            pltpu.make_async_remote_copy(
                src_ref=stage.at[to], dst_ref=landed.at[nt - k], send_sem=t_send.at[number],
                recv_sem=t_recv.at[number], device_id={"tm": to}, device_id_type=MESH).start()
        landed[0] = stage[me_t]

    def all_of(buf, sem):
        view = buf.at[pl.ds(1, nt - 1)]
        pltpu.make_async_copy(view, view, sem).wait()

    def t_mix(number):
        stage, landed, mixed, back = bufs_t[number]
        all_of(landed, t_recv.at[number])

        def block(b, carry):
            lanes = pl.ds(pl.multiple_of(b * LANES, LANES), LANES)
            y = landed[:, :, lanes]
            total = row[0] * y
            for m in range(1, nt):
                total = total + row[m] * jnp.concatenate([y[m:], y[:m]], axis=0)
            mixed[:, :, lanes] = total
            return carry

        lax.fori_loop(0, landed.shape[2] // LANES, block, 0)
        for k in far_first:
            to = lax.rem(me_t + k, nt)
            pltpu.make_async_remote_copy(
                src_ref=mixed.at[k], dst_ref=back.at[me_t], send_sem=b_send.at[number],
                recv_sem=b_recv.at[number], device_id={"tm": to}, device_id_type=MESH).start()
        back[me_t] = mixed[0]

    def t_finish(number, rows_ref):
        stage, landed, mixed, back = bufs_t[number]
        all_of(back, b_recv.at[number])
        piece = stage.shape[1]
        for k in range(nt):
            rows_ref[piece * k:piece * (k + 1), :] = back[k]
        return rows_ref[...]

    def trace_copy(number, side):
        to = lax.rem(me_s + (parts - 1 if side == 0 else 1), parts)
        return pltpu.make_async_remote_copy(
            src_ref=trace_out.at[number, side], dst_ref=trace_in.at[number, 1 - side],
            send_sem=h_send.at[number, side], recv_sem=h_recv.at[number, 1 - side],
            device_id={"space": to}, device_id_type=MESH)

    def s_start(number, v, e_name):
        hi, lo = split(v)
        chosen = mat(e_name)
        t_hi, t_lo = dot(chosen, hi).astype(bf16), dot(chosen, lo).astype(bf16)
        table = jnp.concatenate(
            [lane_cat([t[16 * f:16 * f + 16, columns * i:columns * (i + 1)] for f in range(6)])
             for t in (t_hi, t_lo) for i in range(5)], axis=0)
        packed = dot(table, pick[...])
        packed = packed[:80] + packed[80:]
        for side in range(2):
            trace_out[number, side] = packed[:, slots * side:slots * (side + 1)]
            trace_copy(number, side).start()
        return table

    def flux(v, jac_at, d_name):
        w = []
        for a in range(3):
            total = jac_at[5 * a] * v[:, 0:columns][None]
            for i in range(1, 5):
                total = total + jac_at[5 * a + i] * v[:, columns * i:columns * (i + 1)][None]
            w.append(lane_cat([total[j] for j in range(5)]))
        return dot(mat(d_name), split_rows(jnp.concatenate(w, axis=0)))

    def s_local(table):
        jump = dot(table, jump_w[...])
        return jump[:80] + jump[80:]

    def s_finish(number, jump, et_name):
        for side in range(2):
            trace_copy(number, side).wait_recv()
        hi, lo = split(lane_cat([trace_in[number, 0], trace_in[number, 1]]))
        far = dot(jnp.concatenate([hi, lo], axis=0), far_w[...])
        jump = jump + far[:80] + far[80:]
        put = jnp.concatenate(
            [lane_cat([jump[16 * i:16 * i + 16, columns * f:columns * (f + 1)] for i in range(5)])
             for f in range(6)], axis=0)
        hi, lo = split(put)
        return dot(mat(et_name), jnp.concatenate([hi, lo], axis=0))

    v = lane_cat([adj[i] for i in range(5)])
    t_start(0, v)
    fetch(4).wait()
    rows768 = lax.broadcasted_iota(jnp.int32, (faces, 2 * slots), 0)
    pick[...] = jnp.where(rows768 == send_ref[...], 1.0, 0.0).astype(bf16)
    fetch(8).wait()
    table = s_start(0, v, "e4")
    fetch(5).wait()
    row_id = lax.broadcasted_iota(jnp.int32, (faces, columns), 0)
    lane_id = lax.broadcasted_iota(jnp.int32, (faces, columns), 1)
    far_id = lax.broadcasted_iota(jnp.int32, (2 * slots, columns), 0) + faces
    for f in range(6):
        source = face_ref[f:f + 1, :]
        own = jnp.where(row_id == lane_id + f * columns, 1.0, 0.0)
        jump_w[:, columns * f:columns * (f + 1)] = (own - jnp.where(row_id == source, 1.0, 0.0)).astype(bf16)
        far_w[:, columns * f:columns * (f + 1)] = jnp.where(far_id == source, -1.0, 0.0).astype(bf16)
    for i in (2, 1, 3, 6):
        fetch(i).wait()
    tau = lane_cat([tau_ref[...]] * 5)
    g = lane_cat([grad[i] for i in range(5)])
    part = flux(v, jac, "d4")
    t_mix(0)
    jump = s_local(table)
    part = g - part - s_finish(0, jump, "et4")

    def to_mid(c, carry):
        picked = lane_cat([jac[c, j] for j in range(5)])
        small = dot(mat("q34"), split_rows(picked))
        for j in range(5):
            jm[c, j] = small[:, columns * j:columns * (j + 1)]
        return carry

    lax.fori_loop(0, 15, to_mid, 0)
    owners = owner_ref[...]
    heads = max(8, parts)
    owner_id = lax.broadcasted_iota(jnp.int32, (heads, columns), 0)
    named = jnp.where(owner_id == owners, 1.0, 0.0)
    lane_c = lax.broadcasted_iota(jnp.int32, (columns, LANES), 1)
    sub_c = lax.broadcasted_iota(jnp.int32, (columns, LANES), 0)
    earlier = jnp.where(sub_c < lane_c, 1.0, 0.0).astype(bf16)
    rank = jnp.sum(dot(named.astype(bf16), earlier) * named, axis=0, keepdims=True)
    wide = pack_w.shape[1]
    slot_id = lax.broadcasted_iota(jnp.int32, (wide, columns), 0).astype(f32)
    slot = rank + (me_s * cap).astype(f32)
    for q in range(parts):
        pack_w[q] = jnp.where(jnp.logical_and(slot_id == slot, owners == q), 1.0, 0.0).astype(bf16)

    smoothed = v + tau * (part - t_finish(0, rows_f))

    t_start(1, dot(mat("r43"), split_rows(smoothed)))
    table = s_start(1, smoothed, "e4")
    part = flux(smoothed, jac, "d4")
    t_mix(1)
    jump = s_local(table)
    part = g - part - s_finish(1, jump, "et4")
    rhs = dot(mat("r43"), split_rows(part)) - t_finish(1, rows_m)

    def to_low(x):
        x = dot(mat("r32"), split_rows(x))[:8]
        return jnp.concatenate([x[:, columns * i:columns * (i + 1)] for i in range(5)], axis=0)

    def from_low(x):
        x = lane_cat([x[8 * i:8 * i + 8] for i in range(5)])
        head = x.astype(bf16).astype(f32)
        return dot(mat("p32"), jnp.concatenate([head, head, x - head], axis=0).astype(bf16))

    def low_start(number, x):
        extra = rows_l.shape[0] - 40
        if extra:
            x = jnp.concatenate([x, jnp.zeros((extra, columns), f32)], axis=0)
        t_start(number, x)

    c = tau * rhs
    t_start(3, c)
    table = s_start(2, c, "e3")
    part = flux(c, jm, "d3")
    t_mix(3)
    jump = s_local(table)
    part = rhs - part - s_finish(2, jump, "et3")
    c = c + tau * (part - t_finish(3, rows_m))

    low_start(5, to_low(c))
    table = s_start(3, c, "e3")
    t_start(4, c)
    part = flux(c, jm, "d3")
    t_mix(5)
    jump = s_local(table)
    part = rhs - part - s_finish(3, jump, "et3")

    low = to_low(part) - t_finish(5, rows_l)[:40]
    hi, lo = split(low)
    stacked = jnp.concatenate([hi, lo], axis=0)

    def packed_for(q):
        both = lax.dot_general(
            stacked, pack_w[q], (((1,), (1,)), ((), ())), preferred_element_type=f32)
        return both[:40] + both[40:]

    def low_copy(k):
        return pltpu.make_async_remote_copy(
            src_ref=low_out.at[k], dst_ref=low_in.at[parts - k], send_sem=c_send.at[k],
            recv_sem=c_recv.at[parts - k], device_id={"space": lax.rem(me_s + k, parts)}, device_id_type=MESH)

    def back_copy(k):
        return pltpu.make_async_remote_copy(
            src_ref=sol, dst_ref=low_back.at[parts - k], send_sem=g_send.at[k],
            recv_sem=g_recv.at[parts - k], device_id={"space": lax.rem(me_s + k, parts)}, device_id_type=MESH)

    for k in range(1, parts):
        low_out[k] = packed_for(lax.rem(me_s + k, parts))
        low_copy(k).start()
    t_start(2, smoothed)
    t_mix(4)
    arrived = packed_for(me_s)
    for k in range(1, parts):
        low_copy(k).wait_recv()
    for k in range(1, parts):
        arrived = arrived + low_in[k]
    fetch(7).wait()
    arrived = arrived[:, :cols]
    if wide > cols:
        sol[:, cols:] = jnp.zeros((40, wide - cols), f32)
    for i in range(40):
        sol[i:i + 1, :cols] = jnp.sum(inv[i] * arrived, axis=0, keepdims=True)
    for k in range(1, parts):
        back_copy(k).start()

    def unpacked(values, q):
        v_hi, v_lo = split(values)
        both = dot(jnp.concatenate([v_hi, v_lo], axis=0), pack_w[q])
        return both[:40] + both[40:]

    t_mix(2)
    fix = unpacked(sol[...], me_s)
    for k in range(1, parts):
        back_copy(k).wait_recv()
    for k in range(1, parts):
        fix = fix + unpacked(low_back[k], lax.rem(me_s + k, parts))

    low_start(6, fix)
    c = c + from_low(fix)
    table = s_start(4, c, "e3")
    part = flux(c, jm, "d3")
    t_mix(6)
    jump = s_local(table)
    part = rhs - t_finish(4, rows_m) - part - s_finish(4, jump, "et3")
    c = c + tau * (part - from_low(t_finish(6, rows_l)[:40]))

    t_start(7, c)
    corrected = smoothed + dot(mat("p43"), split_rows(c))
    table = s_start(5, corrected, "e4")
    part = flux(corrected, jac, "d4")
    t_mix(7)
    jump = s_local(table)
    part = g - part - s_finish(5, jump, "et4")
    part = part - t_finish(2, rows_f)
    coupled = dot(mat("p43"), split_rows(t_finish(7, rows_m)))
    result = corrected + tau * (part - coupled)
    for i in range(5):
        out[i] = result[:, columns * i:columns * (i + 1)]

    for number, bufs in enumerate(bufs_t):
        all_of(bufs[0], t_send.at[number])
        all_of(bufs[2], b_send.at[number])
    for number in range(6):
        for side in range(2):
            trace_copy(number, side).wait_send()
    for k in range(1, parts):
        low_copy(k).wait_send()
        back_copy(k).wait_send()


def on_device(nt, parts, where, table, row, adjoint, gradient, jacobian, pseudo_step, send_list,
              face_source, coarse_owner, coarse_inv):
    columns = adjoint.shape[-1]
    cols = coarse_inv.shape[-1]
    slots = send_list.shape[0] // 2
    wide = -(-cols // LANES) * LANES
    width = 5 * columns
    faces = 6 * columns
    operands = (
        adjoint.reshape(5, 64, columns),
        gradient.reshape(5, 64, columns),
        jacobian.reshape(15, 5, 64, columns),
        pseudo_step,
        send_list.reshape(1, 2 * slots),
        face_source,
        coarse_owner.reshape(1, columns),
        coarse_inv.reshape(40, 40, cols),
        jnp.asarray(table),
    )

    low_piece = -(-40 // nt)

    def time_buffers(piece, lanes):
        return [pltpu.VMEM((nt, piece, lanes), f32) for _ in range(4)]

    scratch = [pltpu.VMEM(x.shape, x.dtype) for x in operands]
    scratch += [
        pltpu.SemaphoreType.DMA((len(operands),)),
        pltpu.VMEM((15, 5, 32, columns), f32),
        pltpu.VMEM((faces, 2 * slots), bf16),
        pltpu.VMEM((faces, faces), bf16),
        pltpu.VMEM((2 * slots, faces), bf16),
        pltpu.VMEM((parts, wide, columns), bf16),
        pltpu.VMEM((64, width), f32),
        pltpu.VMEM((32, width), f32),
        pltpu.VMEM((low_piece * nt, columns), f32),
        pltpu.VMEM((40, wide), f32),
    ]
    fine, mid, low = (64 // nt, width), (32 // nt, width), (low_piece, columns)
    for piece, lanes in (fine, mid, fine, mid, mid, low, low, mid):
        scratch += time_buffers(piece, lanes)
    scratch += [
        pltpu.VMEM((6, 2, 80, slots), f32),
        pltpu.VMEM((6, 2, 80, slots), f32),
        pltpu.VMEM((parts, 40, wide), f32),
        pltpu.VMEM((parts, 40, wide), f32),
        pltpu.VMEM((parts, 40, wide), f32),
    ]
    dma = pltpu.SemaphoreType.DMA
    scratch += [dma((8,)) for _ in range(4)] + [dma((6, 2)) for _ in range(2)]
    scratch += [dma((parts,)) for _ in range(4)]
    result = pl.pallas_call(
        functools.partial(kernel, nt, parts, cols // parts, where, row),
        out_shape=jax.ShapeDtypeStruct((5, 64, columns), f32),
        in_specs=[pl.BlockSpec(memory_space=pltpu.HBM)] * len(operands),
        out_specs=pl.BlockSpec(memory_space=pltpu.VMEM),
        scratch_shapes=scratch,
        compiler_params=pltpu.CompilerParams(
            collective_id=0, has_side_effects=True, vmem_limit_bytes=63 * 1024 * 1024),
    )(*operands)
    return result.reshape(adjoint.shape)


def solution(mesh):
    nt, parts = mesh.shape["tm"], mesh.shape["space"]
    where, table = constants()
    placed = (
        P("tm", None, None, None, None, "space"),
        P("tm", None, None, None, None, "space"),
        P("tm", None, None, None, None, None, None, "space"),
        P("tm", "space"),
        P("space"),
        P(None, "space"),
        P("space", None),
        P("tm", None, None, "space"),
    )
    return jax.shard_map(
        functools.partial(on_device, nt, parts, where, table, coupling_row(nt)),
        mesh=mesh,
        in_specs=placed,
        out_specs=P("tm", None, None, None, None, "space"),
        check_vma=False,
    )
```

```python
import functools

import jax
import jax.numpy as jnp
import ml_dtypes
import numpy as np
from jax import lax
from jax.experimental import pallas as pl
from jax.experimental.pallas import tpu as pltpu
from jax.sharding import PartitionSpec as P

MESH = pl.DeviceIdType.MESH
f32, bf16 = jnp.float32, jnp.bfloat16
LANES = 128


def node_points(n):
    return np.linspace(-1.0, 1.0, n)


def lagrange(anchor, target):
    matrix = np.ones((len(target), len(anchor)))
    for c in range(len(anchor)):
        for k in range(len(anchor)):
            if k != c:
                matrix[:, c] = matrix[:, c] * (target - anchor[k]) / (anchor[c] - anchor[k])
    return matrix


def derivative(n):
    points = node_points(n)
    weights = np.ones(n)
    for j in range(n):
        for k in range(n):
            if k != j:
                weights[j] = weights[j] / (points[j] - points[k])
    matrix = np.zeros((n, n))
    for i in range(n):
        for j in range(n):
            if i != j:
                matrix[i, j] = weights[j] / weights[i] / (points[i] - points[j])
        matrix[i, i] = -np.sum(matrix[i])
    return matrix


def coupling_row(count):
    row = []
    for k in range(count):
        d = 0.0 if k == 0 else 0.5 * (-1) ** k * np.cos(np.pi * k / count) / np.sin(np.pi * k / count)
        row.append(float(0.25 * d + 2.0 * ((k == 0) - 1.0 / count)))
    return row


def kron3(a, b, c):
    return np.kron(np.kron(a, b), c)


def pad_to(matrix, rows, cols):
    out = np.zeros((rows, cols))
    out[: matrix.shape[0], : matrix.shape[1]] = matrix
    return out


def split_cat(matrix):
    hi = matrix.astype(np.float32).astype(ml_dtypes.bfloat16)
    lo = (matrix.astype(np.float32) - hi.astype(np.float32)).astype(ml_dtypes.bfloat16)
    return np.concatenate([hi, lo, hi], axis=1)


def face_select(n, rows):
    select = np.zeros((96, rows))
    for f in range(6):
        axis, end = f // 2, (f % 2) * (n - 1)
        count = 0
        for r in range(n):
            for s in range(n):
                index = [r, s]
                index.insert(axis, end)
                select[16 * f + count, (index[0] * n + index[1]) * n + index[2]] = 1.0
                count += 1
    return select


def deriv_cat(n, rows):
    dt, one = derivative(n).T, np.eye(n)
    return np.concatenate(
        [pad_to(m, rows, rows) for m in (kron3(dt, one, one), kron3(one, dt, one), kron3(one, one, dt))],
        axis=1,
    )


@functools.cache
def constants():
    p43 = lagrange(node_points(3), node_points(4))
    p32 = lagrange(node_points(2), node_points(3))
    q34 = lagrange(node_points(4), node_points(3))
    p43k, p32k, q34k = kron3(p43, p43, p43), kron3(p32, p32, p32), kron3(q34, q34, q34)
    e4, e3 = face_select(4, 64), face_select(3, 32)
    tables = {
        "e4": e4,
        "e3": e3,
        "d4": split_cat(deriv_cat(4, 64)),
        "d3": split_cat(deriv_cat(3, 32)),
        "et4": np.concatenate([e4.T, e4.T], axis=1),
        "et3": np.concatenate([e3.T, e3.T], axis=1),
        "r43": split_cat(pad_to(p43k.T, 32, 64)),
        "p43": split_cat(pad_to(p43k, 64, 32)),
        "r32": split_cat(pad_to(p32k.T, 16, 32)),
        "p32": split_cat(pad_to(p32k, 32, 8)),
        "q34": split_cat(pad_to(q34k, 32, 64)),
    }
    where, pieces, at = {}, [], 0
    for name, table in tables.items():
        where[name] = (at, table.shape[0], table.shape[1])
        pieces.append(pad_to(table.astype(np.float64), table.shape[0], 640))
        at += table.shape[0]
    return where, np.concatenate(pieces, axis=0).astype(ml_dtypes.bfloat16)


def dot(a, b):
    return jnp.dot(a, b, preferred_element_type=f32)


def split(x):
    hi = x.astype(bf16)
    return hi, (x - hi.astype(f32)).astype(bf16)


def split_rows(x):
    hi, lo = split(x)
    return jnp.concatenate([hi, hi, lo], axis=0)


def lane_cat(parts):
    return jnp.concatenate(parts, axis=1)


def kernel(nt, parts, cap, where, row, *refs):
    sources, out, held = refs[:9], refs[9], refs[10:19]
    adj, grad, jac, tau_ref, send_ref, face_ref, owner_ref, inv, const = held
    in_sem = refs[19]
    (jm, pick, jump_w, far_w, pack_w, rows_f, rows_m, rows_l, sol, *rest) = refs[20:]
    bufs_t = [rest[4 * i:4 * i + 4] for i in range(8)]
    trace_out, trace_in, low_out, low_in, low_back = rest[32:37]
    t_send, t_recv, b_send, b_recv, h_send, h_recv, c_send, c_recv, g_send, g_recv = rest[37:]
    me_t, me_s = lax.axis_index("tm"), lax.axis_index("space")
    holders, first = nt // 2, nt // 4
    held_id = me_t - first
    is_holder = jnp.logical_and(held_id >= 0, held_id < holders)
    columns = LANES
    width = 5 * columns
    slots = send_ref.shape[1] // 2
    faces = 6 * columns
    cols = inv.shape[2]

    far_first = sorted(range(1, nt), key=lambda k: (-min(k, nt - k), k))

    def mat(name):
        at, height, wide = where[name]
        return const[at:at + height, 0:wide]

    def fetch(i):
        return pltpu.make_async_copy(sources[i], held[i], in_sem.at[i])

    for i in (0, 4, 8, 5, 2, 1, 3, 6, 7):
        fetch(i).start()
    barrier = pltpu.get_barrier_semaphore()
    for k in range(1, nt):
        pl.semaphore_signal(barrier, inc=1, device_id={"tm": lax.rem(me_t + k, nt)}, device_id_type=MESH)
    for k in range(1, parts):
        pl.semaphore_signal(barrier, inc=1, device_id={"space": lax.rem(me_s + k, parts)}, device_id_type=MESH)
    fetch(0).wait()
    pl.semaphore_wait(barrier, nt - 1 + parts - 1)

    def t_start(number, v):
        stage, landed, mixed, back = bufs_t[number]
        piece = stage.shape[1]
        for h in range(holders):
            stage[h] = v[piece * h:piece * (h + 1), :]
        for k in range(holders):
            h = lax.rem(me_t + k, holders)
            to = first + h

            @pl.when(to != me_t)
            def _(h=h, to=to):
                pltpu.make_async_remote_copy(
                    src_ref=stage.at[h], dst_ref=landed.at[lax.rem(me_t - to + nt, nt)],
                    send_sem=t_send.at[number], recv_sem=t_recv.at[number],
                    device_id={"tm": to}, device_id_type=MESH).start()

        @pl.when(is_holder)
        def _():
            landed[0] = stage[held_id]

    def take(buf, count, sem):
        view = buf.at[pl.ds(0, count)]
        pltpu.make_async_copy(view, view, sem).wait()

    def take_holders(buf, sem):
        @pl.when(is_holder)
        def _():
            take(buf, holders - 1, sem)

        @pl.when(jnp.logical_not(is_holder))
        def _():
            take(buf, holders, sem)

    def t_mix(number):
        stage, landed, mixed, back = bufs_t[number]

        @pl.when(is_holder)
        def _():
            take(landed, nt - 1, t_recv.at[number])

            def block(b, carry):
                lanes = pl.ds(pl.multiple_of(b * LANES, LANES), LANES)
                y = landed[:, :, lanes]
                total = row[0] * y
                for m in range(1, nt):
                    total = total + row[m] * jnp.concatenate([y[m:], y[:m]], axis=0)
                mixed[:, :, lanes] = total
                return carry

            lax.fori_loop(0, landed.shape[2] // LANES, block, 0)
            for k in far_first:
                to = lax.rem(me_t + k, nt)
                pltpu.make_async_remote_copy(
                    src_ref=mixed.at[k], dst_ref=back.at[held_id], send_sem=b_send.at[number],
                    recv_sem=b_recv.at[number], device_id={"tm": to}, device_id_type=MESH).start()
            back[held_id] = mixed[0]

    def t_finish(number, rows_ref):
        stage, landed, mixed, back = bufs_t[number]
        take_holders(back, b_recv.at[number])
        piece = stage.shape[1]
        for h in range(holders):
            rows_ref[piece * h:piece * (h + 1), :] = back[h]
        return rows_ref[...]

    def trace_copy(number, side):
        to = lax.rem(me_s + (parts - 1 if side == 0 else 1), parts)
        return pltpu.make_async_remote_copy(
            src_ref=trace_out.at[number, side], dst_ref=trace_in.at[number, 1 - side],
            send_sem=h_send.at[number, side], recv_sem=h_recv.at[number, 1 - side],
            device_id={"space": to}, device_id_type=MESH)

    def s_start(number, v, e_name):
        hi, lo = split(v)
        chosen = mat(e_name)
        t_hi, t_lo = dot(chosen, hi).astype(bf16), dot(chosen, lo).astype(bf16)
        table = jnp.concatenate(
            [lane_cat([t[16 * f:16 * f + 16, columns * i:columns * (i + 1)] for f in range(6)])
             for t in (t_hi, t_lo) for i in range(5)], axis=0)
        packed = dot(table, pick[...])
        packed = packed[:80] + packed[80:]
        for side in range(2):
            trace_out[number, side] = packed[:, slots * side:slots * (side + 1)]
            trace_copy(number, side).start()
        return table

    def flux(v, jac_at, d_name):
        w = []
        for a in range(3):
            total = jac_at[5 * a] * v[:, 0:columns][None]
            for i in range(1, 5):
                total = total + jac_at[5 * a + i] * v[:, columns * i:columns * (i + 1)][None]
            w.append(lane_cat([total[j] for j in range(5)]))
        return dot(mat(d_name), split_rows(jnp.concatenate(w, axis=0)))

    def s_local(table):
        jump = dot(table, jump_w[...])
        return jump[:80] + jump[80:]

    def s_finish(number, jump, et_name):
        for side in range(2):
            trace_copy(number, side).wait_recv()
        hi, lo = split(lane_cat([trace_in[number, 0], trace_in[number, 1]]))
        far = dot(jnp.concatenate([hi, lo], axis=0), far_w[...])
        jump = jump + far[:80] + far[80:]
        put = jnp.concatenate(
            [lane_cat([jump[16 * i:16 * i + 16, columns * f:columns * (f + 1)] for i in range(5)])
             for f in range(6)], axis=0)
        hi, lo = split(put)
        return dot(mat(et_name), jnp.concatenate([hi, lo], axis=0))

    v = lane_cat([adj[i] for i in range(5)])
    t_start(0, v)
    fetch(4).wait()
    rows768 = lax.broadcasted_iota(jnp.int32, (faces, 2 * slots), 0)
    pick[...] = jnp.where(rows768 == send_ref[...], 1.0, 0.0).astype(bf16)
    fetch(8).wait()
    table = s_start(0, v, "e4")
    fetch(5).wait()
    row_id = lax.broadcasted_iota(jnp.int32, (faces, columns), 0)
    lane_id = lax.broadcasted_iota(jnp.int32, (faces, columns), 1)
    far_id = lax.broadcasted_iota(jnp.int32, (2 * slots, columns), 0) + faces
    for f in range(6):
        source = face_ref[f:f + 1, :]
        own = jnp.where(row_id == lane_id + f * columns, 1.0, 0.0)
        jump_w[:, columns * f:columns * (f + 1)] = (own - jnp.where(row_id == source, 1.0, 0.0)).astype(bf16)
        far_w[:, columns * f:columns * (f + 1)] = jnp.where(far_id == source, -1.0, 0.0).astype(bf16)
    for i in (2, 1, 3, 6):
        fetch(i).wait()
    tau = lane_cat([tau_ref[...]] * 5)
    g = lane_cat([grad[i] for i in range(5)])
    part = flux(v, jac, "d4")
    t_mix(0)
    jump = s_local(table)
    part = g - part - s_finish(0, jump, "et4")

    def to_mid(c, carry):
        picked = lane_cat([jac[c, j] for j in range(5)])
        small = dot(mat("q34"), split_rows(picked))
        for j in range(5):
            jm[c, j] = small[:, columns * j:columns * (j + 1)]
        return carry

    lax.fori_loop(0, 15, to_mid, 0)
    owners = owner_ref[...]
    heads = max(8, parts)
    owner_id = lax.broadcasted_iota(jnp.int32, (heads, columns), 0)
    named = jnp.where(owner_id == owners, 1.0, 0.0)
    lane_c = lax.broadcasted_iota(jnp.int32, (columns, LANES), 1)
    sub_c = lax.broadcasted_iota(jnp.int32, (columns, LANES), 0)
    earlier = jnp.where(sub_c < lane_c, 1.0, 0.0).astype(bf16)
    rank = jnp.sum(dot(named.astype(bf16), earlier) * named, axis=0, keepdims=True)
    wide = pack_w.shape[1]
    slot_id = lax.broadcasted_iota(jnp.int32, (wide, columns), 0).astype(f32)
    slot = rank + (me_s * cap).astype(f32)
    for q in range(parts):
        pack_w[q] = jnp.where(jnp.logical_and(slot_id == slot, owners == q), 1.0, 0.0).astype(bf16)

    smoothed = v + tau * (part - t_finish(0, rows_f))

    t_start(1, dot(mat("r43"), split_rows(smoothed)))
    table = s_start(1, smoothed, "e4")
    part = flux(smoothed, jac, "d4")
    t_mix(1)
    jump = s_local(table)
    part = g - part - s_finish(1, jump, "et4")
    rhs = dot(mat("r43"), split_rows(part)) - t_finish(1, rows_m)

    def to_low(x):
        x = dot(mat("r32"), split_rows(x))[:8]
        return jnp.concatenate([x[:, columns * i:columns * (i + 1)] for i in range(5)], axis=0)

    def from_low(x):
        x = lane_cat([x[8 * i:8 * i + 8] for i in range(5)])
        head = x.astype(bf16).astype(f32)
        return dot(mat("p32"), jnp.concatenate([head, head, x - head], axis=0).astype(bf16))

    def low_start(number, x):
        extra = rows_l.shape[0] - 40
        if extra:
            x = jnp.concatenate([x, jnp.zeros((extra, columns), f32)], axis=0)
        t_start(number, x)

    c = tau * rhs
    t_start(3, c)
    table = s_start(2, c, "e3")
    part = flux(c, jm, "d3")
    t_mix(3)
    jump = s_local(table)
    part = rhs - part - s_finish(2, jump, "et3")
    c = c + tau * (part - t_finish(3, rows_m))

    low_start(5, to_low(c))
    table = s_start(3, c, "e3")
    t_start(4, c)
    part = flux(c, jm, "d3")
    t_mix(5)
    jump = s_local(table)
    part = rhs - part - s_finish(3, jump, "et3")

    low = to_low(part) - t_finish(5, rows_l)[:40]
    hi, lo = split(low)
    stacked = jnp.concatenate([hi, lo], axis=0)

    def packed_for(q):
        both = lax.dot_general(
            stacked, pack_w[q], (((1,), (1,)), ((), ())), preferred_element_type=f32)
        return both[:40] + both[40:]

    def low_copy(k):
        return pltpu.make_async_remote_copy(
            src_ref=low_out.at[k], dst_ref=low_in.at[parts - k], send_sem=c_send.at[k],
            recv_sem=c_recv.at[parts - k], device_id={"space": lax.rem(me_s + k, parts)}, device_id_type=MESH)

    def back_copy(k):
        return pltpu.make_async_remote_copy(
            src_ref=sol, dst_ref=low_back.at[parts - k], send_sem=g_send.at[k],
            recv_sem=g_recv.at[parts - k], device_id={"space": lax.rem(me_s + k, parts)}, device_id_type=MESH)

    for k in range(1, parts):
        low_out[k] = packed_for(lax.rem(me_s + k, parts))
        low_copy(k).start()
    t_start(2, smoothed)
    t_mix(4)
    arrived = packed_for(me_s)
    for k in range(1, parts):
        low_copy(k).wait_recv()
    for k in range(1, parts):
        arrived = arrived + low_in[k]
    fetch(7).wait()
    arrived = arrived[:, :cols]
    if wide > cols:
        sol[:, cols:] = jnp.zeros((40, wide - cols), f32)
    for i in range(40):
        sol[i:i + 1, :cols] = jnp.sum(inv[i] * arrived, axis=0, keepdims=True)
    for k in range(1, parts):
        back_copy(k).start()

    def unpacked(values, q):
        v_hi, v_lo = split(values)
        both = dot(jnp.concatenate([v_hi, v_lo], axis=0), pack_w[q])
        return both[:40] + both[40:]

    t_mix(2)
    fix = unpacked(sol[...], me_s)
    for k in range(1, parts):
        back_copy(k).wait_recv()
    for k in range(1, parts):
        fix = fix + unpacked(low_back[k], lax.rem(me_s + k, parts))

    low_start(6, fix)
    c = c + from_low(fix)
    table = s_start(4, c, "e3")
    part = flux(c, jm, "d3")
    t_mix(6)
    jump = s_local(table)
    part = rhs - t_finish(4, rows_m) - part - s_finish(4, jump, "et3")
    c = c + tau * (part - from_low(t_finish(6, rows_l)[:40]))

    t_start(7, c)
    corrected = smoothed + dot(mat("p43"), split_rows(c))
    table = s_start(5, corrected, "e4")
    part = flux(corrected, jac, "d4")
    t_mix(7)
    jump = s_local(table)
    part = g - part - s_finish(5, jump, "et4")
    part = part - t_finish(2, rows_f)
    coupled = dot(mat("p43"), split_rows(t_finish(7, rows_m)))
    result = corrected + tau * (part - coupled)
    for i in range(5):
        out[i] = result[:, columns * i:columns * (i + 1)]

    for number, bufs in enumerate(bufs_t):
        take_holders(bufs[0], t_send.at[number])

        @pl.when(is_holder)
        def _(number=number, bufs=bufs):
            take(bufs[2], nt - 1, b_send.at[number])

    for number in range(6):
        for side in range(2):
            trace_copy(number, side).wait_send()
    for k in range(1, parts):
        low_copy(k).wait_send()
        back_copy(k).wait_send()


def on_device(nt, parts, where, table, row, adjoint, gradient, jacobian, pseudo_step, send_list,
              face_source, coarse_owner, coarse_inv):
    columns = adjoint.shape[-1]
    cols = coarse_inv.shape[-1]
    slots = send_list.shape[0] // 2
    wide = -(-cols // LANES) * LANES
    width = 5 * columns
    faces = 6 * columns
    operands = (
        adjoint.reshape(5, 64, columns),
        gradient.reshape(5, 64, columns),
        jacobian.reshape(15, 5, 64, columns),
        pseudo_step,
        send_list.reshape(1, 2 * slots),
        face_source,
        coarse_owner.reshape(1, columns),
        coarse_inv.reshape(40, 40, cols),
        jnp.asarray(table),
    )

    holders = nt // 2
    low_piece = -(-40 // holders)

    def time_buffers(piece, lanes):
        return [pltpu.VMEM((count, piece, lanes), f32) for count in (holders, nt, nt, holders)]

    scratch = [pltpu.VMEM(x.shape, x.dtype) for x in operands]
    scratch += [
        pltpu.SemaphoreType.DMA((len(operands),)),
        pltpu.VMEM((15, 5, 32, columns), f32),
        pltpu.VMEM((faces, 2 * slots), bf16),
        pltpu.VMEM((faces, faces), bf16),
        pltpu.VMEM((2 * slots, faces), bf16),
        pltpu.VMEM((parts, wide, columns), bf16),
        pltpu.VMEM((64, width), f32),
        pltpu.VMEM((32, width), f32),
        pltpu.VMEM((low_piece * holders, columns), f32),
        pltpu.VMEM((40, wide), f32),
    ]
    fine, mid, low = (64 // holders, width), (32 // holders, width), (low_piece, columns)
    for piece, lanes in (fine, mid, fine, mid, mid, low, low, mid):
        scratch += time_buffers(piece, lanes)
    scratch += [
        pltpu.VMEM((6, 2, 80, slots), f32),
        pltpu.VMEM((6, 2, 80, slots), f32),
        pltpu.VMEM((parts, 40, wide), f32),
        pltpu.VMEM((parts, 40, wide), f32),
        pltpu.VMEM((parts, 40, wide), f32),
    ]
    dma = pltpu.SemaphoreType.DMA
    scratch += [dma((8,)) for _ in range(4)] + [dma((6, 2)) for _ in range(2)]
    scratch += [dma((parts,)) for _ in range(4)]
    result = pl.pallas_call(
        functools.partial(kernel, nt, parts, cols // parts, where, row),
        out_shape=jax.ShapeDtypeStruct((5, 64, columns), f32),
        in_specs=[pl.BlockSpec(memory_space=pltpu.HBM)] * len(operands),
        out_specs=pl.BlockSpec(memory_space=pltpu.VMEM),
        scratch_shapes=scratch,
        compiler_params=pltpu.CompilerParams(
            collective_id=0, has_side_effects=True, vmem_limit_bytes=63 * 1024 * 1024),
    )(*operands)
    return result.reshape(adjoint.shape)


def solution(mesh):
    nt, parts = mesh.shape["tm"], mesh.shape["space"]
    where, table = constants()
    placed = (
        P("tm", None, None, None, None, "space"),
        P("tm", None, None, None, None, "space"),
        P("tm", None, None, None, None, None, None, "space"),
        P("tm", "space"),
        P("space"),
        P(None, "space"),
        P("space", None),
        P("tm", None, None, "space"),
    )
    return jax.shard_map(
        functools.partial(on_device, nt, parts, where, table, coupling_row(nt)),
        mesh=mesh,
        in_specs=placed,
        out_specs=P("tm", None, None, None, None, "space"),
        check_vma=False,
    )
```

```python
import functools

import jax
import jax.numpy as jnp
import ml_dtypes
import numpy as np
from jax import lax
from jax.experimental import pallas as pl
from jax.experimental.pallas import tpu as pltpu
from jax.sharding import PartitionSpec as P

MESH = pl.DeviceIdType.MESH
f32, bf16 = jnp.float32, jnp.bfloat16
LANES = 128


def node_points(n):
    return np.linspace(-1.0, 1.0, n)


def lagrange(anchor, target):
    matrix = np.ones((len(target), len(anchor)))
    for c in range(len(anchor)):
        for k in range(len(anchor)):
            if k != c:
                matrix[:, c] = matrix[:, c] * (target - anchor[k]) / (anchor[c] - anchor[k])
    return matrix


def derivative(n):
    points = node_points(n)
    weights = np.ones(n)
    for j in range(n):
        for k in range(n):
            if k != j:
                weights[j] = weights[j] / (points[j] - points[k])
    matrix = np.zeros((n, n))
    for i in range(n):
        for j in range(n):
            if i != j:
                matrix[i, j] = weights[j] / weights[i] / (points[i] - points[j])
        matrix[i, i] = -np.sum(matrix[i])
    return matrix


def coupling_row(count):
    row = []
    for k in range(count):
        d = 0.0 if k == 0 else 0.5 * (-1) ** k * np.cos(np.pi * k / count) / np.sin(np.pi * k / count)
        row.append(float(0.25 * d + 2.0 * ((k == 0) - 1.0 / count)))
    return row


def kron3(a, b, c):
    return np.kron(np.kron(a, b), c)


def pad_to(matrix, rows, cols):
    out = np.zeros((rows, cols))
    out[: matrix.shape[0], : matrix.shape[1]] = matrix
    return out


def split_cat(matrix):
    hi = matrix.astype(np.float32).astype(ml_dtypes.bfloat16)
    lo = (matrix.astype(np.float32) - hi.astype(np.float32)).astype(ml_dtypes.bfloat16)
    return np.concatenate([hi, lo, hi], axis=1)


def face_select(n, rows):
    select = np.zeros((96, rows))
    for f in range(6):
        axis, end = f // 2, (f % 2) * (n - 1)
        count = 0
        for r in range(n):
            for s in range(n):
                index = [r, s]
                index.insert(axis, end)
                select[16 * f + count, (index[0] * n + index[1]) * n + index[2]] = 1.0
                count += 1
    return select


def deriv_cat(n, rows):
    dt, one = derivative(n).T, np.eye(n)
    return np.concatenate(
        [pad_to(m, rows, rows) for m in (kron3(dt, one, one), kron3(one, dt, one), kron3(one, one, dt))],
        axis=1,
    )


@functools.cache
def constants():
    p43 = lagrange(node_points(3), node_points(4))
    p32 = lagrange(node_points(2), node_points(3))
    q34 = lagrange(node_points(4), node_points(3))
    p43k, p32k, q34k = kron3(p43, p43, p43), kron3(p32, p32, p32), kron3(q34, q34, q34)
    e4, e3 = face_select(4, 64), face_select(3, 32)
    tables = {
        "e4": e4,
        "e3": e3,
        "d4": split_cat(deriv_cat(4, 64)),
        "d3": split_cat(deriv_cat(3, 32)),
        "et4": np.concatenate([e4.T, e4.T], axis=1),
        "et3": np.concatenate([e3.T, e3.T], axis=1),
        "r43": split_cat(pad_to(p43k.T, 32, 64)),
        "p43": split_cat(pad_to(p43k, 64, 32)),
        "r32": split_cat(pad_to(p32k.T, 16, 32)),
        "p32": split_cat(pad_to(p32k, 32, 8)),
        "q34": split_cat(pad_to(q34k, 32, 64)),
    }
    where, pieces, at = {}, [], 0
    for name, table in tables.items():
        where[name] = (at, table.shape[0], table.shape[1])
        pieces.append(pad_to(table.astype(np.float64), table.shape[0], 640))
        at += table.shape[0]
    return where, np.concatenate(pieces, axis=0).astype(ml_dtypes.bfloat16)


def dot(a, b):
    return jnp.dot(a, b, preferred_element_type=f32)


def split(x):
    hi = x.astype(bf16)
    return hi, (x - hi.astype(f32)).astype(bf16)


def split_rows(x):
    hi, lo = split(x)
    return jnp.concatenate([hi, hi, lo], axis=0)


def lane_cat(parts):
    return jnp.concatenate(parts, axis=1)


def kernel(nt, parts, cap, where, row, *refs):
    sources, out, held = refs[:9], refs[9], refs[10:19]
    adj, grad, jac, tau_ref, send_ref, face_ref, owner_ref, inv, const = held
    in_sem = refs[19]
    (jm, pick, jump_w, far_w, pack_w, rows_f, rows_m, rows_l, sol, *rest) = refs[20:]
    bufs_t = [rest[4 * i:4 * i + 4] for i in range(8)]
    trace_out, trace_in, low_out, low_in, low_back = rest[32:37]
    t_send, t_recv, b_send, b_recv, h_send, h_recv, c_send, c_recv, g_send, g_recv = rest[37:]
    me_t, me_s = lax.axis_index("tm"), lax.axis_index("space")
    holders, first = nt // 2, nt // 4
    held_id = me_t - first
    is_holder = jnp.logical_and(held_id >= 0, held_id < holders)
    columns = LANES
    width = 5 * columns
    slots = send_ref.shape[1] // 2
    faces = 6 * columns
    cols = inv.shape[2]

    far_first = sorted(range(1, nt), key=lambda k: (-min(k, nt - k), k))

    def mat(name):
        at, height, wide = where[name]
        return const[at:at + height, 0:wide]

    def fetch(i):
        return pltpu.make_async_copy(sources[i], held[i], in_sem.at[i])

    for i in (0, 4, 8, 5, 2, 1, 3, 6, 7):
        fetch(i).start()
    barrier = pltpu.get_barrier_semaphore()
    for k in range(1, nt):
        pl.semaphore_signal(barrier, inc=1, device_id={"tm": lax.rem(me_t + k, nt)}, device_id_type=MESH)
    for k in range(1, parts):
        pl.semaphore_signal(barrier, inc=1, device_id={"space": lax.rem(me_s + k, parts)}, device_id_type=MESH)
    fetch(0).wait()
    pl.semaphore_wait(barrier, nt - 1 + parts - 1)

    def t_start(number, v):
        stage, landed, mixed, back = bufs_t[number]
        piece = stage.shape[1]
        for h in range(holders):
            stage[h] = v[piece * h:piece * (h + 1), :]
        for k in range(holders):
            h = lax.rem(me_t + k, holders)
            to = first + h

            @pl.when(to != me_t)
            def _(h=h, to=to):
                pltpu.make_async_remote_copy(
                    src_ref=stage.at[h], dst_ref=landed.at[lax.rem(me_t - to + nt, nt)],
                    send_sem=t_send.at[number], recv_sem=t_recv.at[number],
                    device_id={"tm": to}, device_id_type=MESH).start()

        @pl.when(is_holder)
        def _():
            landed[0] = stage[held_id]

    def take(buf, count, sem):
        view = buf.at[pl.ds(0, count)]
        pltpu.make_async_copy(view, view, sem).wait()

    def take_holders(buf, sem):
        @pl.when(is_holder)
        def _():
            take(buf, holders - 1, sem)

        @pl.when(jnp.logical_not(is_holder))
        def _():
            take(buf, holders, sem)

    def t_mix(number):
        stage, landed, mixed, back = bufs_t[number]

        @pl.when(is_holder)
        def _():
            take(landed, nt - 1, t_recv.at[number])

            def block(b, carry):
                lanes = pl.ds(pl.multiple_of(b * LANES, LANES), LANES)
                y = landed[:, :, lanes]
                total = row[0] * y
                for m in range(1, nt):
                    total = total + row[m] * jnp.concatenate([y[m:], y[:m]], axis=0)
                mixed[:, :, lanes] = total
                return carry

            lax.fori_loop(0, landed.shape[2] // LANES, block, 0)
            for k in far_first:
                to = lax.rem(me_t + k, nt)
                pltpu.make_async_remote_copy(
                    src_ref=mixed.at[k], dst_ref=back.at[held_id], send_sem=b_send.at[number],
                    recv_sem=b_recv.at[number], device_id={"tm": to}, device_id_type=MESH).start()
            back[held_id] = mixed[0]

    def t_finish(number, rows_ref):
        stage, landed, mixed, back = bufs_t[number]
        take_holders(back, b_recv.at[number])
        piece = stage.shape[1]
        for h in range(holders):
            rows_ref[piece * h:piece * (h + 1), :] = back[h]
        return rows_ref[...]

    def trace_copy(number, side):
        to = lax.rem(me_s + (parts - 1 if side == 0 else 1), parts)
        return pltpu.make_async_remote_copy(
            src_ref=trace_out.at[number, side], dst_ref=trace_in.at[number, 1 - side],
            send_sem=h_send.at[number, side], recv_sem=h_recv.at[number, 1 - side],
            device_id={"space": to}, device_id_type=MESH)

    def s_start(number, v, e_name):
        hi, lo = split(v)
        chosen = mat(e_name)
        t_hi, t_lo = dot(chosen, hi).astype(bf16), dot(chosen, lo).astype(bf16)
        table = jnp.concatenate(
            [lane_cat([t[16 * f:16 * f + 16, columns * i:columns * (i + 1)] for f in range(6)])
             for t in (t_hi, t_lo) for i in range(5)], axis=0)
        packed = dot(table, pick[...])
        packed = packed[:80] + packed[80:]
        for side in range(2):
            trace_out[number, side] = packed[:, slots * side:slots * (side + 1)]
            trace_copy(number, side).start()
        return table

    def flux(v, jac_at, d_name):
        w = []
        for a in range(3):
            total = jac_at[5 * a] * v[:, 0:columns][None]
            for i in range(1, 5):
                total = total + jac_at[5 * a + i] * v[:, columns * i:columns * (i + 1)][None]
            w.append(lane_cat([total[j] for j in range(5)]))
        return dot(mat(d_name), split_rows(jnp.concatenate(w, axis=0)))

    def s_local(table):
        jump = dot(table, jump_w[...])
        return jump[:80] + jump[80:]

    def s_finish(number, jump, et_name):
        for side in range(2):
            trace_copy(number, side).wait_recv()
        hi, lo = split(lane_cat([trace_in[number, 0], trace_in[number, 1]]))
        far = dot(jnp.concatenate([hi, lo], axis=0), far_w[...])
        jump = jump + far[:80] + far[80:]
        put = jnp.concatenate(
            [lane_cat([jump[16 * i:16 * i + 16, columns * f:columns * (f + 1)] for i in range(5)])
             for f in range(6)], axis=0)
        hi, lo = split(put)
        return dot(mat(et_name), jnp.concatenate([hi, lo], axis=0))

    v = lane_cat([adj[i] for i in range(5)])
    t_start(0, v)
    fetch(4).wait()
    rows768 = lax.broadcasted_iota(jnp.int32, (faces, 2 * slots), 0)
    pick[...] = jnp.where(rows768 == send_ref[...], 1.0, 0.0).astype(bf16)
    fetch(8).wait()
    table = s_start(0, v, "e4")
    fetch(5).wait()
    row_id = lax.broadcasted_iota(jnp.int32, (faces, columns), 0)
    lane_id = lax.broadcasted_iota(jnp.int32, (faces, columns), 1)
    far_id = lax.broadcasted_iota(jnp.int32, (2 * slots, columns), 0) + faces
    for f in range(6):
        source = face_ref[f:f + 1, :]
        own = jnp.where(row_id == lane_id + f * columns, 1.0, 0.0)
        jump_w[:, columns * f:columns * (f + 1)] = (own - jnp.where(row_id == source, 1.0, 0.0)).astype(bf16)
        far_w[:, columns * f:columns * (f + 1)] = jnp.where(far_id == source, -1.0, 0.0).astype(bf16)
    for i in (2, 1, 3, 6):
        fetch(i).wait()
    tau = lane_cat([tau_ref[...]] * 5)
    g = lane_cat([grad[i] for i in range(5)])
    part = flux(v, jac, "d4")
    t_mix(0)
    jump = s_local(table)
    part = g - part - s_finish(0, jump, "et4")

    def to_mid(c, carry):
        picked = lane_cat([jac[c, j] for j in range(5)])
        small = dot(mat("q34"), split_rows(picked))
        for j in range(5):
            jm[c, j] = small[:, columns * j:columns * (j + 1)]
        return carry

    lax.fori_loop(0, 15, to_mid, 0)
    owners = owner_ref[...]
    heads = max(8, parts)
    owner_id = lax.broadcasted_iota(jnp.int32, (heads, columns), 0)
    named = jnp.where(owner_id == owners, 1.0, 0.0)
    lane_c = lax.broadcasted_iota(jnp.int32, (columns, LANES), 1)
    sub_c = lax.broadcasted_iota(jnp.int32, (columns, LANES), 0)
    earlier = jnp.where(sub_c < lane_c, 1.0, 0.0).astype(bf16)
    rank = jnp.sum(dot(named.astype(bf16), earlier) * named, axis=0, keepdims=True)
    wide = pack_w.shape[1]
    slot_id = lax.broadcasted_iota(jnp.int32, (wide, columns), 0).astype(f32)
    slot = rank + (me_s * cap).astype(f32)
    for q in range(parts):
        pack_w[q] = jnp.where(jnp.logical_and(slot_id == slot, owners == q), 1.0, 0.0).astype(bf16)

    smoothed = v + tau * (part - t_finish(0, rows_f))

    t_start(1, dot(mat("r43"), split_rows(smoothed)))
    table = s_start(1, smoothed, "e4")
    part = flux(smoothed, jac, "d4")
    t_mix(1)
    jump = s_local(table)
    part = g - part - s_finish(1, jump, "et4")
    rhs = dot(mat("r43"), split_rows(part)) - t_finish(1, rows_m)

    def to_low(x):
        x = dot(mat("r32"), split_rows(x))[:8]
        return jnp.concatenate([x[:, columns * i:columns * (i + 1)] for i in range(5)], axis=0)

    def from_low(x):
        x = lane_cat([x[8 * i:8 * i + 8] for i in range(5)])
        head = x.astype(bf16).astype(f32)
        return dot(mat("p32"), jnp.concatenate([head, head, x - head], axis=0).astype(bf16))

    def low_start(number, x):
        extra = rows_l.shape[0] - 40
        if extra:
            x = jnp.concatenate([x, jnp.zeros((extra, columns), f32)], axis=0)
        t_start(number, x)

    c = tau * rhs
    t_start(3, c)
    table = s_start(2, c, "e3")
    part = flux(c, jm, "d3")
    t_mix(3)
    jump = s_local(table)
    part = rhs - part - s_finish(2, jump, "et3")
    c = c + tau * (part - t_finish(3, rows_m))

    low_start(5, to_low(c))
    table = s_start(3, c, "e3")
    part = flux(c, jm, "d3")
    t_mix(5)
    jump = s_local(table)
    part = rhs - part - s_finish(3, jump, "et3")

    low = to_low(part) - t_finish(5, rows_l)[:40]
    hi, lo = split(low)
    stacked = jnp.concatenate([hi, lo], axis=0)

    def packed_for(q):
        both = lax.dot_general(
            stacked, pack_w[q], (((1,), (1,)), ((), ())), preferred_element_type=f32)
        return both[:40] + both[40:]

    def low_copy(k):
        return pltpu.make_async_remote_copy(
            src_ref=low_out.at[k], dst_ref=low_in.at[parts - k], send_sem=c_send.at[k],
            recv_sem=c_recv.at[parts - k], device_id={"space": lax.rem(me_s + k, parts)}, device_id_type=MESH)

    def back_copy(k):
        return pltpu.make_async_remote_copy(
            src_ref=sol, dst_ref=low_back.at[parts - k], send_sem=g_send.at[k],
            recv_sem=g_recv.at[parts - k], device_id={"space": lax.rem(me_s + k, parts)}, device_id_type=MESH)

    for k in range(1, parts):
        low_out[k] = packed_for(lax.rem(me_s + k, parts))
        low_copy(k).start()
    t_start(4, c)
    t_start(2, smoothed)
    arrived = packed_for(me_s)
    for k in range(1, parts):
        low_copy(k).wait_recv()
    for k in range(1, parts):
        arrived = arrived + low_in[k]
    fetch(7).wait()
    arrived = arrived[:, :cols]
    if wide > cols:
        sol[:, cols:] = jnp.zeros((40, wide - cols), f32)
    for i in range(40):
        sol[i:i + 1, :cols] = jnp.sum(inv[i] * arrived, axis=0, keepdims=True)
    for k in range(1, parts):
        back_copy(k).start()

    def unpacked(values, q):
        v_hi, v_lo = split(values)
        both = dot(jnp.concatenate([v_hi, v_lo], axis=0), pack_w[q])
        return both[:40] + both[40:]

    t_mix(4)
    fix = unpacked(sol[...], me_s)
    for k in range(1, parts):
        back_copy(k).wait_recv()
    for k in range(1, parts):
        fix = fix + unpacked(low_back[k], lax.rem(me_s + k, parts))

    low_start(6, fix)
    c = c + from_low(fix)
    table = s_start(4, c, "e3")
    part = flux(c, jm, "d3")
    t_mix(6)
    t_mix(2)
    jump = s_local(table)
    part = rhs - t_finish(4, rows_m) - part - s_finish(4, jump, "et3")
    c = c + tau * (part - from_low(t_finish(6, rows_l)[:40]))

    t_start(7, c)
    corrected = smoothed + dot(mat("p43"), split_rows(c))
    table = s_start(5, corrected, "e4")
    part = flux(corrected, jac, "d4")
    t_mix(7)
    jump = s_local(table)
    part = g - part - s_finish(5, jump, "et4")
    part = part - t_finish(2, rows_f)
    coupled = dot(mat("p43"), split_rows(t_finish(7, rows_m)))
    result = corrected + tau * (part - coupled)
    for i in range(5):
        out[i] = result[:, columns * i:columns * (i + 1)]

    for number, bufs in enumerate(bufs_t):
        take_holders(bufs[0], t_send.at[number])

        @pl.when(is_holder)
        def _(number=number, bufs=bufs):
            take(bufs[2], nt - 1, b_send.at[number])

    for number in range(6):
        for side in range(2):
            trace_copy(number, side).wait_send()
    for k in range(1, parts):
        low_copy(k).wait_send()
        back_copy(k).wait_send()


def on_device(nt, parts, where, table, row, adjoint, gradient, jacobian, pseudo_step, send_list,
              face_source, coarse_owner, coarse_inv):
    columns = adjoint.shape[-1]
    cols = coarse_inv.shape[-1]
    slots = send_list.shape[0] // 2
    wide = -(-cols // LANES) * LANES
    width = 5 * columns
    faces = 6 * columns
    operands = (
        adjoint.reshape(5, 64, columns),
        gradient.reshape(5, 64, columns),
        jacobian.reshape(15, 5, 64, columns),
        pseudo_step,
        send_list.reshape(1, 2 * slots),
        face_source,
        coarse_owner.reshape(1, columns),
        coarse_inv.reshape(40, 40, cols),
        jnp.asarray(table),
    )

    holders = nt // 2
    low_piece = -(-40 // holders)

    def time_buffers(piece, lanes):
        return [pltpu.VMEM((count, piece, lanes), f32) for count in (holders, nt, nt, holders)]

    scratch = [pltpu.VMEM(x.shape, x.dtype) for x in operands]
    scratch += [
        pltpu.SemaphoreType.DMA((len(operands),)),
        pltpu.VMEM((15, 5, 32, columns), f32),
        pltpu.VMEM((faces, 2 * slots), bf16),
        pltpu.VMEM((faces, faces), bf16),
        pltpu.VMEM((2 * slots, faces), bf16),
        pltpu.VMEM((parts, wide, columns), bf16),
        pltpu.VMEM((64, width), f32),
        pltpu.VMEM((32, width), f32),
        pltpu.VMEM((low_piece * holders, columns), f32),
        pltpu.VMEM((40, wide), f32),
    ]
    fine, mid, low = (64 // holders, width), (32 // holders, width), (low_piece, columns)
    for piece, lanes in (fine, mid, fine, mid, mid, low, low, mid):
        scratch += time_buffers(piece, lanes)
    scratch += [
        pltpu.VMEM((6, 2, 80, slots), f32),
        pltpu.VMEM((6, 2, 80, slots), f32),
        pltpu.VMEM((parts, 40, wide), f32),
        pltpu.VMEM((parts, 40, wide), f32),
        pltpu.VMEM((parts, 40, wide), f32),
    ]
    dma = pltpu.SemaphoreType.DMA
    scratch += [dma((8,)) for _ in range(4)] + [dma((6, 2)) for _ in range(2)]
    scratch += [dma((parts,)) for _ in range(4)]
    result = pl.pallas_call(
        functools.partial(kernel, nt, parts, cols // parts, where, row),
        out_shape=jax.ShapeDtypeStruct((5, 64, columns), f32),
        in_specs=[pl.BlockSpec(memory_space=pltpu.HBM)] * len(operands),
        out_specs=pl.BlockSpec(memory_space=pltpu.VMEM),
        scratch_shapes=scratch,
        compiler_params=pltpu.CompilerParams(
            collective_id=0, has_side_effects=True, vmem_limit_bytes=63 * 1024 * 1024),
    )(*operands)
    return result.reshape(adjoint.shape)


def solution(mesh):
    nt, parts = mesh.shape["tm"], mesh.shape["space"]
    where, table = constants()
    placed = (
        P("tm", None, None, None, None, "space"),
        P("tm", None, None, None, None, "space"),
        P("tm", None, None, None, None, None, None, "space"),
        P("tm", "space"),
        P("space"),
        P(None, "space"),
        P("space", None),
        P("tm", None, None, "space"),
    )
    return jax.shard_map(
        functools.partial(on_device, nt, parts, where, table, coupling_row(nt)),
        mesh=mesh,
        in_specs=placed,
        out_specs=P("tm", None, None, None, None, "space"),
        check_vma=False,
    )
```
